256 devices in a mesh: row: 8 (over y_hi, x), col: 16 (over y_lo, z), rep: 2 (over core).
Axes of the slice: x: 4, y: 4 (y_hi: 2, y_lo: 2; y = y_hi * 2 + y_lo), z: 8, core: 2. Of those that a mesh axis runs over, the one named last changes fastest.
Arguments:
- tokens: bfloat16 [4096, 5120], P(('col', 'rep'), 'row'), may hold values from -6 to 6
- out_grad: bfloat16 [4096, 5120], P(('col', 'rep'), 'row'), may hold values from -6 to 6
- w_in: bfloat16 [5120, 13824], P('row', 'col'), may hold values from -0.078125 to 0.078125
- bias_in: float32 [13824], P('col'), may hold values from -3 to 3
- w_out: bfloat16 [13824, 5120], P('col', 'row'), may hold values from -0.0546875 to 0.0546875
Outputs:
- input_grad: bfloat16 [4096, 5120], P(('col', 'rep'), 'row')
- w_in_grad: bfloat16 [5120, 13824], P('row', ('col', 'rep'))
- bias_grad: float32 [13824], P(('col', 'rep'))
- w_out_grad: bfloat16 [13824, 5120], P(('col', 'rep'), 'row')
The draws below stay inside these ranges and needn't reach their ends.
All inputs are finite; a program needn't handle non-finite values.
Results may differ from the reference program's by a relative error of at most 0.03.
Values may be sent and summed in bfloat16 or wider, within the bound.
A program may use at most 64 MiB of HBM per device.

```python
import jax
import jax.numpy as jnp
from jax import lax

D = 5120
FF = 13824
TOK_DEV = 128
TOKENS = 4096
N_ROW = 8
N_COL = 16
N_REP = 2


def levels(own_key, shape, split, smallest, high):
    def one(axis_at, shards_of):
        steps = jax.random.uniform(jax.random.fold_in(jax.random.fold_in(own_key, 6), axis_at), (shards_of,), jnp.float32, smallest / len(split), high / len(split))
        return jnp.repeat(jnp.exp(steps), shape[axis_at] // shards_of).reshape((-1,) + (1,) * (len(shape) - axis_at - 1))

    gain = one(*split[0])
    for cut in split[1:]:
        gain = gain * one(*cut)
    return gain


def bell_draw(rng, extent, spread, bound, shards=(), dtype=jnp.bfloat16):
    loudness = levels(rng, extent, shards, -0.22, 0.18) if shards else 1.0
    values = jax.random.normal(rng, extent, jnp.float32) * spread * loudness
    return jnp.minimum(jnp.maximum(values, -bound), bound).astype(dtype)


def setup_inputs(seed: int = 0) -> dict:
    splits = jax.random.split(jax.random.key(seed), 6)
    return {
        "tokens": bell_draw(splits[0], (TOKENS, D), 1.0, 6.0, ((0, 32), (1, 8))),
        "out_grad": bell_draw(splits[1], (TOKENS, D), 1.0, 6.0, ((0, 32), (1, 8))),
        "w_in": bell_draw(splits[2], (D, FF), D ** -0.5, 0.078125, ((0, 8), (1, 16))),
        "bias_in": bell_draw(splits[3], (FF,), 0.5, 3.0, ((0, 16),), jnp.float32),
        "w_out": bell_draw(splits[4], (FF, D), FF ** -0.5, 0.0546875, ((0, 16), (1, 8))),
    }


def act_fn(value):
    return jax.nn.gelu(value, approximate=True)

def to_bf16(value):
    return lax.optimization_barrier(value.astype(jnp.bfloat16)).astype(jnp.float32)

def reference(tokens, out_grad, w_in, bias_in, w_out):
    width = D // N_ROW
    pre = jnp.zeros((TOKENS, FF), jnp.float32)
    back = jnp.zeros((TOKENS, FF), jnp.float32)
    for block in range(N_ROW):
        lower = block * width
        part_pre = jnp.dot(tokens[:, lower:lower + width], w_in[lower:lower + width], preferred_element_type=jnp.float32)
        part_back = jnp.dot(out_grad[:, lower:lower + width], w_out[:, lower:lower + width].T, preferred_element_type=jnp.float32)
        pre = pre + to_bf16(part_pre)
        back = back + to_bf16(part_back)
    pre = pre + bias_in.astype(jnp.float32)[None, :]
    activation, pullback = jax.vjp(act_fn, pre)
    pre_grad = pullback(back)[0].astype(jnp.bfloat16)
    activation = activation.astype(jnp.bfloat16)
    factor = 1.0 / jnp.sqrt(jnp.float32(TOKENS))
    groups = TOKENS // (TOK_DEV * N_REP)
    tok_sets = tokens.reshape(groups, N_REP, TOK_DEV, D)
    grad_sets = pre_grad.reshape(groups, N_REP, TOK_DEV, FF)
    act_sets = activation.reshape(groups, N_REP, TOK_DEV, FF)
    og_sets = out_grad.reshape(groups, N_REP, TOK_DEV, D)
    w_in_acc = jnp.zeros((D, FF), jnp.float32)
    w_out_acc = jnp.zeros((FF, D), jnp.float32)
    bias_acc = jnp.zeros((FF,), jnp.float32)
    for member in range(N_REP):
        x_set = tok_sets[:, member].reshape(groups * TOK_DEV, D)
        g_set = grad_sets[:, member].reshape(groups * TOK_DEV, FF)
        a_set = act_sets[:, member].reshape(groups * TOK_DEV, FF)
        o_set = og_sets[:, member].reshape(groups * TOK_DEV, D)
        w_in_acc = w_in_acc + to_bf16(jnp.dot(x_set.T, g_set, preferred_element_type=jnp.float32) * factor)
        w_out_acc = w_out_acc + to_bf16(jnp.dot(a_set.T, o_set, preferred_element_type=jnp.float32) * factor)
        bias_acc = bias_acc + to_bf16(lax.optimization_barrier(jnp.sum(g_set.astype(jnp.float32), axis=0)) * factor)
    hid = FF // N_COL
    input_acc = jnp.zeros((TOKENS, D), jnp.float32)
    for block in range(N_COL):
        lower = block * hid
        part = jnp.dot(pre_grad[:, lower:lower + hid], w_in[:, lower:lower + hid].T, preferred_element_type=jnp.float32)
        input_acc = input_acc + to_bf16(part)
    return (input_acc.astype(jnp.bfloat16), w_in_acc.astype(jnp.bfloat16), bias_acc, w_out_acc.astype(jnp.bfloat16))
```

```python
import jax
import jax.numpy as jnp
from jax import lax
from jax.experimental import pallas as pl
from jax.experimental.pallas import tpu as pltpu
from jax.sharding import PartitionSpec as P

MESH = pl.DeviceIdType.MESH
BF16, F32 = jnp.bfloat16, jnp.float32
NX, NZ = 4, 8
GROUP, HALF = 128, 64
WIDTH, WIDE = 640, 1280
HID, HALF_HID = 864, 432
QUARTER, EIGHTH = 32, 16
CHUNKS = 8
SCALE = 1.0 / 64.0
ORDER = (
    [(0, slot) for slot in range(CHUNKS)]
    + [(1, slot) for slot in (0, 1, 2, 3, 7, 6, 5, 4)]
)


def contract(a, b, dim_a, dim_b):
    return lax.dot_general(
        a, b, (((dim_a,), (dim_b,)), ((), ())), preferred_element_type=F32
    )


def gelu_parts(value):
    cube = value * value * value
    bend = jnp.tanh(0.7978845608 * (value + 0.044715 * cube))
    return bend


def kernel(
    tok, og, win, bias, wout,
    ig_out, wgi_out, bg_out, wgo_out,
    xg, wi, wo, bias_v, part, first, second_out, second, ap, pre,
    ig, zr, ys, yr, wg, core_out, core_in, far_out, far_in,
    bsum, bcore, bpair, bfar,
    local_sem, send_sem, recv_sem,
):
    row, col, rep = lax.axis_index("row"), lax.axis_index("col"), lax.axis_index("rep")
    yh, x = row // NX, row % NX
    yl, z = col // NZ, col % NZ

    def at(yh_=yh, x_=x, yl_=yl, z_=z, rep_=rep):
        return {"row": yh_ * NX + x_, "col": yl_ * NZ + z_, "rep": rep_}

    x_right, x_left = at(x_=(x + 1) % NX), at(x_=(x + 3) % NX)
    z_right, z_left = at(z_=(z + 1) % NZ), at(z_=(z + 7) % NZ)
    core = at(rep_=1 - rep)
    y_far = at(yh_=1 - yh)
    y_peers = [
        (yh, 1 - yl, at(yl_=1 - yl)),
        (1 - yh, yl, y_far),
        (1 - yh, 1 - yl, at(yh_=1 - yh, yl_=1 - yl)),
    ]

    counts = {"local": 0, "remote": 0}
    sent = []

    def move(src, dst):
        copy = pltpu.make_async_copy(src, dst, local_sem.at[counts["local"]])
        counts["local"] += 1
        copy.start()
        return copy

    def send(src, dst, device):
        number = counts["remote"]
        counts["remote"] += 1
        copy = pltpu.make_async_remote_copy(
            src_ref=src,
            dst_ref=dst,
            send_sem=send_sem.at[number],
            recv_sem=recv_sem.at[number],
            device_id=device,
            device_id_type=MESH,
        )
        copy.start()
        sent.append(copy)
        return copy

    def span(start, size, unit):
        return pl.ds(pl.multiple_of(start, unit), size)

    my_rows = span(yl * HALF, HALF, HALF)
    my_lanes = span(yh * WIDTH, WIDTH, 128)
    far_lanes = span((1 - yh) * WIDTH, WIDTH, 128)

    own_x = move(tok.at[span(yh * HALF, HALF, HALF)], xg.at[0, 0, my_rows, my_lanes])
    own_g = move(og.at[span(yh * HALF, HALF, HALF)], xg.at[1, 0, my_rows, my_lanes])
    own_wi = move(win, wi.at[my_lanes])
    own_wo = move(wout, wo.at[:, my_lanes])
    own_bias = move(bias, bias_v)

    barrier = pltpu.get_barrier_semaphore()
    everyone = [x_right, x_left, z_right, z_left, core] + [p[2] for p in y_peers]
    for device in everyone:
        pl.semaphore_signal(barrier, inc=1, device_id=device, device_id_type=MESH)
    pl.semaphore_wait(barrier, len(everyone))

    def spread(j, source):
        return [
            send(
                source.at[span(to_yh * HALF, HALF, HALF)],
                xg.at[j, 0, my_rows, my_lanes],
                device,
            )
            for to_yh, _, device in y_peers
        ]

    ring = {}

    def ring_start(j):
        ring[j, 1] = [send(xg.at[j, 0], xg.at[j, 1], z_right)]
        ring[j, 2] = [send(xg.at[j, 0], xg.at[j, 2], z_left)]

    here = set()

    def arrive(j, slot):
        if slot == 0 or (j, slot) in here:
            return
        here.add((j, slot))
        for copy in ring[j, slot]:
            copy.wait_recv()

    def forward(j, slot):
        arrive(j, slot)
        device = z_right if slot % 2 else z_left
        if slot < 5:
            ring[j, slot + 2] = [send(xg.at[j, slot], xg.at[j, slot + 2], device)]
        else:
            rows = pl.ds(0 if slot == 5 else HALF, HALF)
            ring.setdefault((j, 7), []).append(
                send(xg.at[j, slot, rows], xg.at[j, 7, rows], device)
            )

    x_parts = spread(0, tok)
    half_w = span(rep * (WIDTH // 2), WIDTH // 2, 16)
    wi_mine = span(yh * WIDTH + rep * (WIDTH // 2), WIDTH // 2, 16)
    wi_theirs = span((1 - yh) * WIDTH + rep * (WIDTH // 2), WIDTH // 2, 16)
    wi_copy = send(win.at[half_w], wi.at[wi_mine], y_far)
    half_h = span(rep * HALF_HID, HALF_HID, 16)

    own_x.wait()
    for copy in x_parts:
        copy.wait_recv()
    ring_start(0)
    g_parts = spread(1, og)
    wo_copy = send(wout.at[half_h], wo.at[half_h, my_lanes], y_far)

    wi_copy.wait_recv()
    wi_core = send(wi.at[wi_theirs], wi.at[wi_theirs], core)
    forward(0, 1)
    forward(0, 2)
    own_wi.wait()
    own_bias.wait()
    wi_core.wait_recv()

    stage1, stage2, stage3, stage4 = {}, {}, {}, {}

    def quarter(of, offset=0, size=QUARTER):
        return span(((x + of) % NX) * QUARTER + offset, size, EIGHTH)

    def run1(k):
        j, slot = ORDER[k]
        arrive(j, slot)
        if j == 0:
            product = contract(xg[0, slot], wi[...], 1, 0)
        else:
            product = contract(xg[1, slot], wo[...], 1, 1)
        part[k] = product.astype(BF16)
        stage1[k] = [
            send(part.at[k, quarter(2, 0, EIGHTH)], first.at[k, 0], x_right),
            send(part.at[k, quarter(2, EIGHTH, EIGHTH)], first.at[k, 1], x_left),
        ]

    def run2(k):
        stage1[k][0].wait_recv()
        low, high = pl.ds(0, EIGHTH), pl.ds(EIGHTH, EIGHTH)
        second_out[k, 0, low] = (
            part[k, quarter(1, 0, EIGHTH)].astype(F32) + first[k, 0].astype(F32)
        ).astype(BF16)
        second_out[k, 0, high] = part[k, quarter(1, EIGHTH, EIGHTH)]
        right = send(second_out.at[k, 0], second.at[k, 0], x_right)
        stage1[k][1].wait_recv()
        second_out[k, 1, high] = (
            part[k, quarter(3, EIGHTH, EIGHTH)].astype(F32) + first[k, 1].astype(F32)
        ).astype(BF16)
        second_out[k, 1, low] = part[k, quarter(3, 0, EIGHTH)]
        left = send(second_out.at[k, 1], second.at[k, 1], x_left)
        stage2[k] = [right, left]

    def run3(k):
        j, slot = ORDER[k]
        for copy in stage2[k]:
            copy.wait_recv()
        total = (
            part[k, quarter(0)].astype(F32)
            + second[k, 0].astype(F32)
            + second[k, 1].astype(F32)
        )
        mine = quarter(0)
        if j == 0:
            value = total + bias_v[...]
            pre[slot] = value
            result = 0.5 * value * (1.0 + gelu_parts(value))
        else:
            value = pre[slot]
            bend = gelu_parts(value)
            slope = 0.7978845608 * (1.0 + 3.0 * 0.044715 * value * value)
            result = total * (
                0.5 * (1.0 + bend) + 0.5 * value * (1.0 - bend * bend) * slope
            )
        ap[j, slot, mine] = result.astype(BF16)
        block = ap.at[j, slot, mine]
        stage3[k] = [send(block, block, x_right), send(block, block, x_left)]

    def run4(k):
        j, slot = ORDER[k]
        stage3[k][0].wait_recv()
        block = ap.at[j, slot, quarter(3, 0, EIGHTH)]
        right = send(block, block, x_right)
        stage3[k][1].wait_recv()
        block = ap.at[j, slot, quarter(1, EIGHTH, EIGHTH)]
        left = send(block, block, x_left)
        stage4[k] = [right, left]

    def run5(k):
        for copy in stage4[k]:
            copy.wait_recv()

    started = set()

    def weight_grad(j, pair):
        slots = pl.ds(2 * pair, 2)
        for slot in (2 * pair, 2 * pair + 1):
            arrive(j, slot)
        left = ap[1 - j, slots].reshape(2 * GROUP, HID)
        right = xg[j, slots].reshape(2 * GROUP, WIDE)
        product = contract(left, right, 0, 0)
        if j in started:
            wg[j] += product
        else:
            started.add(j)
            wg[j] = product

    def bias_part(slot, fresh):
        rows = ap[1, slot].astype(F32).reshape(GROUP // 8, 8, HID).sum(axis=0)
        bsum[...] = rows if fresh else bsum[...] + rows

    def input_part(slot):
        ig[slot] = contract(ap[1, slot], wi[...], 1, 1).astype(BF16)

    core_copy, far_copy = {}, {}

    def core_send(j, far):
        lanes = far_lanes if far else my_lanes
        rows = span((1 - rep) * HALF_HID, HALF_HID, 16)
        core_out[j, far] = (wg[j, rows, lanes] * SCALE).astype(BF16)
        core_copy[j, far] = send(core_out.at[j, far], core_in.at[j, far], core)

    def far_send(j):
        core_copy[j, 1].wait_recv()
        rows = span(rep * HALF_HID, HALF_HID, 16)
        total = wg[j, rows, far_lanes] * SCALE + core_in[j, 1].astype(F32)
        far_out[j] = total.astype(BF16)
        far_copy[j] = send(far_out.at[j], far_in.at[j], y_far)

    def weight_final(j, out):
        core_copy[j, 0].wait_recv()
        far_copy[j].wait_recv()
        rows = span(rep * HALF_HID, HALF_HID, 16)
        total = wg[j, rows, my_lanes] * SCALE + core_in[j, 0].astype(F32)
        out[...] = (total + far_in[j].astype(F32)).astype(out.dtype)

    low, high = pl.ds(0, HALF), pl.ds(HALF, HALF)
    ring_sum = {}

    def sum_send(side, step, slot, rows, add):
        if add:
            ring_sum[side, step - 1, rows.start].wait_recv()
            ig[slot, rows] = (
                ig[slot, rows].astype(F32) + zr[side, step - 1, rows].astype(F32)
            ).astype(BF16)
        ring_sum[side, step, rows.start] = send(
            ig.at[slot, rows], zr.at[side, step, rows], z_left if side else z_right
        )

    for k in range(len(ORDER) + 4):
        if k == 1:
            forward(0, 3)
            forward(0, 4)
        if k == 3:
            forward(0, 5)
            forward(0, 6)
            own_g.wait()
            for copy in g_parts:
                copy.wait_recv()
            ring_start(1)
        if k == 4:
            wo_copy.wait_recv()
            theirs = wo.at[half_h, far_lanes]
            wo_core = send(theirs, theirs, core)
        if k == 6:
            forward(1, 1)
            forward(1, 2)
        if k == 8:
            own_wo.wait()
            wo_core.wait_recv()
            forward(1, 3)
            forward(1, 4)
        if k == 10:
            forward(1, 5)
            forward(1, 6)
        if 4 <= k:
            run5(k - 4)
        if 3 <= k < 19:
            run4(k - 3)
        if 2 <= k < 18:
            run3(k - 2)
        if 1 <= k < 17:
            run2(k - 1)
        if k < 16:
            run1(k)
        if 10 <= k < 14:
            weight_grad(1, k - 10)
        if k == 14:
            core_send(1, 1)
            core_send(1, 0)
        if k == 15:
            far_send(1)
        if k >= 12:
            slot = ORDER[k - 4][1]
            input_part(slot)
            bias_part(slot, k == 12)
        if k == 14:
            weight_grad(0, 0)
        if k == 16:
            weight_grad(0, 1)
            sum_send(0, 0, 7, low, False)
            sum_send(1, 0, 7, high, False)
        if k == 17:
            sum_send(0, 1, 6, high, False)
            sum_send(0, 1, 6, low, True)
            weight_grad(0, 3)
        if k == 18:
            sum_send(1, 1, 5, low, False)
            sum_send(1, 1, 5, high, True)
        if k == 19:
            sum_send(0, 2, 4, high, True)
            sum_send(0, 2, 4, low, True)
            weight_grad(0, 2)

    core_bias = send(bsum, bcore, core)
    core_send(0, 1)
    core_send(0, 0)
    sum_send(1, 2, 3, low, True)
    sum_send(1, 2, 3, high, True)
    far_send(0)
    core_bias.wait_recv()
    bpair[...] = bsum[...] + bcore[...]
    far_bias = send(bpair, bfar, y_far)
    sum_send(0, 3, 2, high, True)
    sum_send(0, 3, 2, low, True)
    sum_send(1, 3, 1, low, True)
    sum_send(1, 3, 1, high, True)
    weight_final(1, wgo_out)
    far_bias.wait_recv()
    total = jnp.sum(bpair[...] + bfar[...], axis=0, keepdims=True) * SCALE
    bg_out[...] = jnp.where(rep == 0, total[:, :HALF_HID], total[:, HALF_HID:])

    for rows in (low, high):
        for side in (0, 1):
            ring_sum[side, 3, rows.start].wait_recv()
        ys[rows] = (
            ig[0, rows].astype(F32)
            + zr[0, 3, rows].astype(F32)
            + zr[1, 3, rows].astype(F32)
        ).astype(BF16)
    back = [
        send(
            ys.at[span(to_yl * HALF, HALF, HALF), span(to_yh * WIDTH, WIDTH, 128)],
            yr.at[yh, yl],
            device,
        )
        for to_yh, to_yl, device in y_peers
    ]
    yr[yh, yl] = ys[my_rows, my_lanes]
    weight_final(0, wgi_out)
    for copy in back:
        copy.wait_recv()
    for half in (0, 1):
        ig_out[pl.ds(half * HALF, HALF)] = (
            yr[half, 0].astype(F32) + yr[half, 1].astype(F32)
        ).astype(BF16)
    for copy in sent:
        copy.wait_send()


def local(tokens, out_grad, w_in, bias_in, w_out):
    hbm, vmem = pl.BlockSpec(memory_space=pl.ANY), pl.BlockSpec(memory_space=pltpu.VMEM)
    steps = len(ORDER)
    ig, wgi, bg, wgo = pl.pallas_call(
        kernel,
        name="ffn_backward",
        out_shape=(
            jax.ShapeDtypeStruct((GROUP, WIDTH), BF16),
            jax.ShapeDtypeStruct((HALF_HID, WIDTH), BF16),
            jax.ShapeDtypeStruct((1, HALF_HID), F32),
            jax.ShapeDtypeStruct((HALF_HID, WIDTH), BF16),
        ),
        in_specs=[hbm] * 5,
        out_specs=(vmem,) * 4,
        scratch_shapes=[
            pltpu.VMEM((2, CHUNKS, GROUP, WIDE), BF16),
            pltpu.VMEM((WIDE, HID), BF16),
            pltpu.VMEM((HID, WIDE), BF16),
            pltpu.VMEM((1, HID), F32),
            pltpu.VMEM((steps, GROUP, HID), BF16),
            pltpu.VMEM((steps, 2, EIGHTH, HID), BF16),
            pltpu.VMEM((steps, 2, QUARTER, HID), BF16),
            pltpu.VMEM((steps, 2, QUARTER, HID), BF16),
            pltpu.VMEM((2, CHUNKS, GROUP, HID), BF16),
            pltpu.VMEM((CHUNKS, QUARTER, HID), F32),
            pltpu.VMEM((CHUNKS, GROUP, WIDE), BF16),
            pltpu.VMEM((2, 4, GROUP, WIDE), BF16),
            pltpu.VMEM((GROUP, WIDE), BF16),
            pltpu.VMEM((2, 2, HALF, WIDTH), BF16),
            pltpu.VMEM((2, HID, WIDE), F32),
            pltpu.VMEM((2, 2, HALF_HID, WIDTH), BF16),
            pltpu.VMEM((2, 2, HALF_HID, WIDTH), BF16),
            pltpu.VMEM((2, HALF_HID, WIDTH), BF16),
            pltpu.VMEM((2, HALF_HID, WIDTH), BF16),
            pltpu.VMEM((8, HID), F32),
            pltpu.VMEM((8, HID), F32),
            pltpu.VMEM((8, HID), F32),
            pltpu.VMEM((8, HID), F32),
            pltpu.SemaphoreType.DMA((5,)),
            pltpu.SemaphoreType.DMA((200,)),
            pltpu.SemaphoreType.DMA((200,)),
        ],
        compiler_params=pltpu.CompilerParams(
            collective_id=0, has_side_effects=True, vmem_limit_bytes=58 << 20
        ),
        cost_estimate=pl.CostEstimate(
            flops=11_300_000_000, bytes_accessed=4_000_000, transcendentals=0
        ),
    )(tokens, out_grad, w_in, bias_in.reshape(1, HID), w_out)
    return ig, wgi.T, bg.reshape(HALF_HID), wgo


def solution(mesh):
    in_specs = (
        P(("col", "rep"), "row"),
        P(("col", "rep"), "row"),
        P("row", "col"),
        P("col"),
        P("col", "row"),
    )
    out_specs = (
        P(("col", "rep"), "row"),
        P("row", ("col", "rep")),
        P(("col", "rep")),
        P(("col", "rep"), "row"),
    )
    return jax.shard_map(local, mesh=mesh, in_specs=in_specs, out_specs=out_specs, check_vma=False)
```

```python
import jax
import jax.numpy as jnp
from jax import lax
from jax.experimental import pallas as pl
from jax.experimental.pallas import tpu as pltpu
from jax.sharding import PartitionSpec as P

MESH = pl.DeviceIdType.MESH
BF16, F32 = jnp.bfloat16, jnp.float32
NX, NZ = 4, 8
GROUP, HALF = 128, 64
WIDTH, WIDE = 640, 1280
HID, CORE_HID = 864, 432
PADDED = 896
PARTS = ((0, 192), (192, 240))
PLACE = (0, 384)
LANES = ((0, 384), (384, 512), (0, 896))
QUARTER, EIGHTH = 32, 16
CHUNKS = 8
SCALE = 1.0 / 64.0
SCHEDULE = (
    ("sx",), ("zs", 0), ("wf", 0, 0), ("zf", 0, 1, 0), ("zf", 0, 2, 1), ("r1", 0, 0, 0), ("zf", 0, 1, 1),
    ("r1", 0, 0, 1), ("zf", 0, 2, 0), ("r1", 0, 0, 2), ("r2", 0, 0, 0), ("wf", 0, 1), ("r2", 0, 0, 1),
    ("zf", 0, 3, 0), ("zf", 0, 4, 1), ("r2", 0, 0, 2), ("r3", 0, 0, 0), ("r1", 0, 1, 0), ("r3", 0, 0, 1),
    ("r1", 0, 1, 1), ("r3", 0, 0, 2), ("zf", 0, 4, 0), ("r4", 0, 0, 0), ("r1", 0, 1, 4), ("zf", 0, 3, 1),
    ("r1", 0, 0, 3), ("r2", 0, 1, 0), ("r1", 0, 0, 4), ("r2", 0, 1, 1), ("r4", 0, 0, 1), ("r4", 0, 0, 2),
    ("r5", 0, 0, 0), ("r1", 0, 1, 3), ("zf", 0, 6, 1), ("zf", 0, 5, 0), ("wf", 1, 0), ("zs", 1),
    ("r3", 0, 1, 0), ("r2", 0, 1, 4), ("r2", 0, 0, 4), ("r2", 0, 0, 3), ("r3", 0, 1, 1), ("r5", 0, 0, 1),
    ("r5", 0, 0, 2), ("r2", 0, 1, 3), ("r4", 0, 1, 0), ("r1", 0, 0, 6), ("r3", 0, 1, 4), ("r3", 0, 0, 4),
    ("r3", 0, 0, 3), ("r4", 0, 1, 1), ("wf", 1, 1), ("r1", 0, 0, 5), ("r3", 0, 1, 3), ("r2", 0, 0, 6),
    ("r5", 0, 1, 0), ("r4", 0, 1, 4), ("r1", 0, 0, 7), ("r4", 0, 0, 4), ("r1", 0, 1, 5), ("zf", 1, 2, 1),
    ("zf", 1, 1, 0), ("r2", 0, 0, 5), ("r1", 0, 1, 6), ("r4", 0, 1, 3), ("r1", 0, 1, 2), ("r5", 0, 1, 4),
    ("r3", 0, 0, 6), ("r2", 0, 0, 7), ("r5", 0, 0, 4), ("r5", 0, 1, 1), ("r4", 0, 0, 3), ("r2", 0, 1, 5),
    ("zf", 1, 1, 1), ("zf", 1, 2, 0), ("wg", 1, 2, 0), ("r3", 0, 0, 5), ("r5", 0, 1, 3), ("r2", 0, 1, 2),
    ("r4", 0, 0, 6), ("r2", 0, 1, 6), ("r3", 0, 0, 7), ("r5", 0, 0, 3), ("zf", 1, 3, 0), ("zf", 1, 4, 1),
    ("r3", 0, 1, 5), ("r4", 0, 0, 5), ("r1", 0, 1, 7), ("r3", 0, 1, 2), ("r5", 0, 0, 6), ("r1", 1, 0, 2),
    ("r1", 1, 0, 1), ("r4", 0, 0, 7), ("zf", 1, 4, 0), ("zf", 1, 3, 1), ("r1", 1, 0, 3), ("r5", 0, 0, 5),
    ("r4", 0, 1, 5), ("r1", 1, 0, 4), ("r2", 0, 1, 7), ("r1", 1, 1, 4), ("r4", 0, 1, 2), ("r2", 1, 0, 1),
    ("r2", 1, 0, 2), ("r5", 0, 0, 7), ("r3", 0, 1, 6), ("zf", 1, 6, 1), ("r2", 1, 0, 3), ("zf", 1, 5, 0),
    ("r5", 0, 1, 5), ("r2", 1, 0, 4), ("r3", 0, 1, 7), ("r2", 1, 1, 4), ("r5", 0, 1, 2), ("wg", 1, 2, 1),
    ("r3", 1, 0, 2), ("r3", 1, 0, 1), ("r4", 0, 1, 6), ("wg", 1, 2, 2), ("r3", 1, 0, 4), ("r4", 0, 1, 7),
    ("r3", 1, 0, 3), ("r3", 1, 1, 4), ("r4", 1, 0, 2), ("r1", 1, 0, 5), ("r1", 1, 0, 6), ("r1", 1, 0, 7),
    ("r4", 1, 0, 4), ("r1", 1, 1, 7), ("r4", 1, 0, 3), ("r1", 1, 1, 6), ("r5", 1, 0, 2), ("r1", 1, 1, 5),
    ("r2", 1, 0, 5), ("r2", 1, 0, 6), ("r2", 1, 0, 7), ("r5", 1, 0, 4), ("r4", 1, 1, 4), ("r4", 1, 0, 1),
    ("r2", 1, 1, 7), ("r5", 1, 0, 3), ("r5", 0, 1, 7), ("r5", 0, 1, 6), ("wg", 1, 2, 3), ("r2", 1, 1, 5),
    ("r3", 1, 0, 5), ("r2", 1, 1, 6), ("r3", 1, 0, 6), ("cs", 1, 1), ("r3", 1, 0, 7), ("r5", 1, 1, 4),
    ("ip", 4), ("r5", 1, 0, 1), ("wg", 0, 0, 1), ("r3", 1, 1, 7), ("cs", 1, 0), ("r1", 1, 0, 0),
    ("r4", 1, 0, 5), ("r1", 1, 1, 2), ("r3", 1, 1, 6), ("fs", 1, 1), ("r4", 1, 0, 6), ("r1", 1, 1, 3),
    ("fs", 1, 0), ("r4", 1, 0, 7), ("r4", 1, 1, 7), ("r3", 1, 1, 5), ("r2", 1, 0, 0), ("r5", 1, 0, 5),
    ("wg", 0, 0, 2), ("r1", 1, 1, 1), ("r1", 1, 1, 0), ("r2", 1, 1, 3), ("r5", 1, 0, 7), ("r4", 1, 1, 6),
    ("r5", 1, 1, 7), ("ip", 7), ("ss", 1, 0, 1), ("r4", 1, 1, 5), ("ss", 0, 0, 0), ("r2", 1, 1, 2),
    ("r3", 1, 0, 0), ("r2", 1, 1, 1), ("bp", 7), ("r5", 1, 0, 6), ("r2", 1, 1, 0), ("wg", 0, 0, 3),
    ("r3", 1, 1, 3), ("r5", 1, 1, 6), ("ip", 6), ("ss", 0, 1, 1), ("bp", 6), ("r5", 1, 1, 5), ("ip", 5),
    ("ss", 1, 1, 0), ("r4", 1, 0, 0), ("r3", 1, 1, 2), ("wg", 0, 1, 2), ("r3", 1, 1, 1), ("ss", 1, 1, 1),
    ("ss", 0, 1, 0), ("r3", 1, 1, 0), ("r4", 1, 1, 3), ("r5", 1, 0, 0), ("wg", 0, 0, 0), ("r4", 1, 1, 2),
    ("cs", 0, 0), ("bp", 5), ("wg", 0, 1, 3), ("r4", 1, 1, 1), ("wo", 1, 0), ("r4", 1, 1, 0),
    ("ss", 0, 2, 1), ("r5", 1, 1, 3), ("ip", 3), ("ss", 1, 2, 0), ("fs", 0, 0), ("r5", 1, 1, 2), ("ip", 2),
    ("r5", 1, 1, 1), ("ip", 1), ("r5", 1, 1, 0), ("ip", 0), ("wg", 0, 1, 0), ("ss", 1, 2, 1),
    ("ss", 0, 2, 0), ("wg", 0, 1, 1), ("cs", 0, 1), ("bp", 3), ("bp", 0), ("bp", 1), ("wo", 1, 1), ("bp", 2),
    ("bp", 4), ("bc",), ("ss", 0, 3, 1), ("ss", 1, 3, 0), ("fs", 0, 1), ("wo", 0, 0), ("bf",),
    ("ss", 0, 3, 0), ("ss", 1, 3, 1), ("wo", 0, 1), ("yb",), ("bo",), ("io",),
)


def contract(a, b, dim_a, dim_b):
    return lax.dot_general(
        a, b, (((dim_a,), (dim_b,)), ((), ())), preferred_element_type=F32
    )


def bend_of(value):
    return jnp.tanh(0.7978845608 * (value + 0.044715 * value * value * value))


def kernel(
    tok, og, win, bias, wout,
    ig_out, wgi_out, bg_out, wgo_out,
    xg, wi, wo, bias_raw, bias_v, part, first, second_out, second, ap, pre,
    ig, zr, ys, yr, wg, core_out, core_in, far_out, far_in,
    bsum, bcore, bpair, bfar,
    local_sem, send_sem, recv_sem,
):
    row, col, rep = lax.axis_index("row"), lax.axis_index("col"), lax.axis_index("rep")
    yh, x = row // NX, row % NX
    yl, z = col // NZ, col % NZ

    def at(yh_=yh, x_=x, yl_=yl, z_=z, rep_=rep):
        return {"row": yh_ * NX + x_, "col": yl_ * NZ + z_, "rep": rep_}

    x_right, x_left = at(x_=(x + 1) % NX), at(x_=(x + 3) % NX)
    z_right, z_left = at(z_=(z + 1) % NZ), at(z_=(z + 7) % NZ)
    core = at(rep_=1 - rep)
    y_far = at(yh_=1 - yh)
    y_peers = [
        (yh, 1 - yl, at(yl_=1 - yl)),
        (1 - yh, yl, y_far),
        (1 - yh, 1 - yl, at(yh_=1 - yh, yl_=1 - yl)),
    ]

    counts = {"local": 0, "remote": 0}
    sent, arrived = [], set()

    def move(src, dst):
        copy = pltpu.make_async_copy(src, dst, local_sem.at[counts["local"]])
        counts["local"] += 1
        copy.start()
        return copy

    def send(src, dst, device):
        number = counts["remote"]
        counts["remote"] += 1
        copy = pltpu.make_async_remote_copy(
            src_ref=src,
            dst_ref=dst,
            send_sem=send_sem.at[number],
            recv_sem=recv_sem.at[number],
            device_id=device,
            device_id_type=MESH,
        )
        copy.start()
        sent.append(copy)
        return copy

    def need(*copies):
        for copy in copies:
            if id(copy) not in arrived:
                arrived.add(id(copy))
                copy.wait_recv()

    def span(start, size, unit):
        return pl.ds(pl.multiple_of(start, unit), size)

    my_rows = span(yl * HALF, HALF, HALF)
    my_lanes = span(yh * WIDTH, WIDTH, 128)
    far_lanes = span((1 - yh) * WIDTH, WIDTH, 128)

    def source_rows(which, of):
        start, size = PARTS[of]
        return span(which * CORE_HID + start, size, 16)

    def held_rows(which, of):
        size = PARTS[of][1]
        return span(PLACE[of] + which * size, size, 16)

    own = {}
    for j, (block, weights, held) in enumerate(((tok, win, wi), (og, wout, wo))):
        own[j] = [
            move(block.at[span(yh * HALF, HALF, HALF)], xg.at[j, 0, my_rows, my_lanes])
        ]
        for of in (0, 1):
            own[j, of] = [
                move(
                    weights.at[pl.ds(which * CORE_HID + PARTS[of][0], PARTS[of][1])],
                    held.at[
                        pl.ds(PLACE[of] + which * PARTS[of][1], PARTS[of][1]), my_lanes
                    ],
                )
                for which in (0, 1)
            ]
    own_bias = [move(bias, bias_raw)]

    def own_ready(key):
        while own[key]:
            own[key].pop().wait()

    own["bias"] = own_bias

    def bias_ready():
        if not own["bias"]:
            return
        own_ready("bias")
        raw = bias_raw[...].reshape(1, HID)
        blocks = [
            raw[:, which * CORE_HID + start : which * CORE_HID + start + size]
            for start, size in PARTS
            for which in (0, 1)
        ]
        blocks.append(jnp.zeros((1, PADDED - HID), F32))
        bias_v[...] = jnp.concatenate(blocks, axis=1)

    for held in (wi, wo):
        held[pl.ds(HID, PADDED - HID)] = jnp.zeros((PADDED - HID, WIDE), BF16)

    barrier = pltpu.get_barrier_semaphore()
    everyone = [x_right, x_left, z_right, z_left, core] + [p[2] for p in y_peers]
    for device in everyone:
        pl.semaphore_signal(barrier, inc=1, device_id=device, device_id_type=MESH)
    pl.semaphore_wait(barrier, len(everyone))

    spread, weight_far, weight_core, ring = {}, {}, {}, {}
    halves = (pl.ds(0, HALF), pl.ds(HALF, HALF))

    def send_block(j):
        source = og if j else tok
        spread[j] = [
            send(
                source.at[span(to_yh * HALF, HALF, HALF)],
                xg.at[j, 0, my_rows, my_lanes],
                device,
            )
            for to_yh, _, device in y_peers
        ]

    def send_weights(j, of):
        source, held = (wout, wo) if j else (win, wi)
        weight_far[j, of] = send(
            source.at[source_rows(rep, of)], held.at[held_rows(rep, of), my_lanes], y_far
        )

    def begin():
        send_block(0)
        send_weights(0, 0)

    def ring_send(j, source, slot, half, device):
        rows = halves[half]
        ring[j, slot, half] = send(xg.at[j, source, rows], xg.at[j, slot, rows], device)

    def ring_start(j):
        own_ready(j)
        need(*spread[j])
        for half in (0, 1):
            ring_send(j, 0, 1, half, z_right)
            ring_send(j, 0, 2, 1 - half, z_left)
        if j == 0:
            send_weights(0, 1)

    def ring_pass(j, slot, half):
        need(ring[j, slot, half])
        ring_send(j, slot, min(slot + 2, 7), half, z_right if slot % 2 else z_left)

    def chunk_ready(j, slot):
        if slot == 0:
            own_ready(j)
            need(*spread[j])
        else:
            need(ring[j, slot, 0], ring[j, slot, 1])

    def weights_pass(j, of):
        need(weight_far[j, of])
        block = (wo if j else wi).at[held_rows(rep, of), far_lanes]
        weight_core[j, of] = send(block, block, core)
        if (j, of) == (0, 0):
            send_block(1)
        if (j, of) == (0, 1):
            send_weights(1, 0)
            send_weights(1, 1)

    def weights_ready(j, lanes):
        for of in (0, 1):
            if lanes in (of, 2):
                own_ready((j, of))
                need(weight_core[j, of])

    stage = {}

    def quarter(of, offset=0, size=QUARTER):
        return span(((x + of) % NX) * QUARTER + offset, size, EIGHTH)

    low16, high16 = pl.ds(0, EIGHTH), pl.ds(EIGHTH, EIGHTH)

    def multiply(j, lanes, slot):
        chunk_ready(j, slot)
        weights_ready(j, lanes)
        at_lanes = pl.ds(*LANES[lanes])
        weights = (wo if j else wi)[at_lanes]
        part[j, slot, :, at_lanes] = contract(xg[j, slot], weights, 1, 1).astype(BF16)
        rows = (quarter(2, 0, EIGHTH), quarter(2, EIGHTH, EIGHTH))
        stage[1, j, lanes, slot] = [
            send(
                part.at[j, slot, rows[side], at_lanes],
                first.at[j, slot, side, :, at_lanes],
                x_left if side else x_right,
            )
            for side in (0, 1)
        ]

    def add_first(j, lanes, slot):
        at_lanes = pl.ds(*LANES[lanes])
        copies = []
        for side in (0, 1):
            need(stage[1, j, lanes, slot][side])
            of = 3 if side else 1
            summed = (high16, EIGHTH) if side else (low16, 0)
            plain = (low16, 0) if side else (high16, EIGHTH)
            second_out[j, slot, side, summed[0], at_lanes] = (
                part[j, slot, quarter(of, summed[1], EIGHTH), at_lanes].astype(F32)
                + first[j, slot, side, :, at_lanes].astype(F32)
            ).astype(BF16)
            second_out[j, slot, side, plain[0], at_lanes] = part[
                j, slot, quarter(of, plain[1], EIGHTH), at_lanes
            ]
            copies.append(
                send(
                    second_out.at[j, slot, side, :, at_lanes],
                    second.at[j, slot, side, :, at_lanes],
                    x_left if side else x_right,
                )
            )
        stage[2, j, lanes, slot] = copies

    def activate(j, lanes, slot):
        need(*stage[2, j, lanes, slot])
        at_lanes = pl.ds(*LANES[lanes])
        mine = quarter(0)
        total = (
            part[j, slot, mine, at_lanes].astype(F32)
            + second[j, slot, 0, :, at_lanes].astype(F32)
            + second[j, slot, 1, :, at_lanes].astype(F32)
        )
        if j == 0:
            bias_ready()
            value = total + bias_v[:, at_lanes]
            pre[slot, :, at_lanes] = value
            result = 0.5 * value * (1.0 + bend_of(value))
        else:
            value = pre[slot, :, at_lanes]
            bend = bend_of(value)
            slope = 0.7978845608 * (1.0 + 3.0 * 0.044715 * value * value)
            result = total * (
                0.5 * (1.0 + bend) + 0.5 * value * (1.0 - bend * bend) * slope
            )
        ap[j, slot, mine, at_lanes] = result.astype(BF16)
        block = ap.at[j, slot, mine, at_lanes]
        stage[3, j, lanes, slot] = [send(block, block, x_right), send(block, block, x_left)]

    def hand_on(j, lanes, slot):
        at_lanes = pl.ds(*LANES[lanes])
        copies = []
        for side in (0, 1):
            need(stage[3, j, lanes, slot][side])
            rows = quarter(1, EIGHTH, EIGHTH) if side else quarter(3, 0, EIGHTH)
            block = ap.at[j, slot, rows, at_lanes]
            copies.append(send(block, block, x_left if side else x_right))
        stage[4, j, lanes, slot] = copies

    def all_here(j, lanes, slot):
        need(*stage[4, j, lanes, slot])

    core_copy, far_copy = {}, {}
    started = set()

    def weight_grad(j, lanes, pair):
        for slot in (2 * pair, 2 * pair + 1):
            chunk_ready(j, slot)
        slots, hidden = pl.ds(2 * pair, 2), pl.ds(*LANES[lanes])
        left = ap[1 - j, slots, :, hidden].reshape(2 * GROUP, LANES[lanes][1])
        right = xg[j, slots].reshape(2 * GROUP, WIDE)
        product = contract(left, right, 0, 0)
        wg[j, hidden] = wg[j, hidden] + product if (j, lanes) in started else product
        started.add((j, lanes))

    def core_send(j, of):
        rows = pl.ds(*PARTS[of])
        for far, lanes in ((1, far_lanes), (0, my_lanes)):
            block = wg[j, held_rows(1 - rep, of), lanes] * SCALE
            core_out[j, far, rows] = block.astype(BF16)
            core_copy[j, of, far] = send(
                core_out.at[j, far, rows], core_in.at[j, far, rows], core
            )

    def far_send(j, of):
        need(core_copy[j, of, 1])
        rows = pl.ds(*PARTS[of])
        block = wg[j, held_rows(rep, of), far_lanes] * SCALE
        far_out[j, rows] = (block + core_in[j, 1, rows].astype(F32)).astype(BF16)
        far_copy[j, of] = send(far_out.at[j, rows], far_in.at[j, rows], y_far)

    def weight_out(j, of):
        need(core_copy[j, of, 0], far_copy[j, of])
        rows = pl.ds(*PARTS[of])
        block = wg[j, held_rows(rep, of), my_lanes] * SCALE
        total = block + core_in[j, 0, rows].astype(F32)
        out = wgo_out if j else wgi_out
        out[rows] = (total + far_in[j, rows].astype(F32)).astype(BF16)

    bias_copy = {}

    def bias_part(slot):
        rows = ap[1, slot].astype(F32).reshape(GROUP // 8, 8, PADDED).sum(axis=0)
        bsum[...] = bsum[...] + rows if "bias" in started else rows
        started.add("bias")

    def bias_core():
        bias_copy[0] = send(bsum, bcore, core)

    def bias_far():
        need(bias_copy[0])
        bpair[...] = bsum[...] + bcore[...]
        bias_copy[1] = send(bpair, bfar, y_far)

    def bias_out():
        need(bias_copy[1])
        total = jnp.sum(bpair[...] + bfar[...], axis=0, keepdims=True) * SCALE
        mine = [
            jnp.concatenate(
                [
                    total[:, PLACE[of] + which * size : PLACE[of] + (which + 1) * size]
                    for of, (_, size) in enumerate(PARTS)
                ],
                axis=1,
            )
            for which in (0, 1)
        ]
        bg_out[...] = jnp.where(rep == 0, mine[0], mine[1])

    ring_sum, back = {}, []

    def input_part(slot):
        ig[slot] = contract(ap[1, slot], wi[...], 1, 0).astype(BF16)

    def sum_pass(side, step, half):
        slot = ((7, 6, 4, 2), (7, 5, 3, 1))[side][step]
        rows = halves[half]
        if (side, step - 1, half) in ring_sum:
            need(ring_sum[side, step - 1, half])
            ig[slot, rows] = (
                ig[slot, rows].astype(F32) + zr[side, step - 1, rows].astype(F32)
            ).astype(BF16)
        ring_sum[side, step, half] = send(
            ig.at[slot, rows], zr.at[side, step, rows], z_left if side else z_right
        )

    def sum_end():
        for half, rows in enumerate(halves):
            need(ring_sum[0, 3, half], ring_sum[1, 3, half])
            ys[rows] = (
                ig[0, rows].astype(F32)
                + zr[0, 3, rows].astype(F32)
                + zr[1, 3, rows].astype(F32)
            ).astype(BF16)
        for to_yh, to_yl, device in y_peers:
            lanes = span(to_yh * WIDTH, WIDTH, 128)
            block = ys.at[span(to_yl * HALF, HALF, HALF), lanes]
            back.append(send(block, yr.at[yh, yl], device))
        yr[yh, yl] = ys[my_rows, my_lanes]

    def input_out():
        need(*back)
        for half, rows in enumerate(halves):
            total = yr[half, 0].astype(F32) + yr[half, 1].astype(F32)
            ig_out[rows] = total.astype(BF16)

    steps = {
        "sx": begin, "zs": ring_start, "zf": ring_pass, "wf": weights_pass,
        "r1": multiply, "r2": add_first, "r3": activate, "r4": hand_on, "r5": all_here,
        "wg": weight_grad, "cs": core_send, "fs": far_send, "wo": weight_out,
        "bp": bias_part, "bc": bias_core, "bf": bias_far, "bo": bias_out,
        "ip": input_part, "ss": sum_pass, "yb": sum_end, "io": input_out,
    }
    for name, *which in SCHEDULE:
        steps[name](*which)
    for copy in sent:
        copy.wait_send()


def hand_over(*refs):
    for source, target in zip(refs[:4], refs[4:]):
        target[...] = source[...]


def local(tokens, out_grad, w_in, bias_in, w_out):
    hbm, vmem = pl.BlockSpec(memory_space=pl.ANY), pl.BlockSpec(memory_space=pltpu.VMEM)
    ig, wgi, bg, wgo = pl.pallas_call(
        kernel,
        name="ffn_backward",
        out_shape=(
            jax.ShapeDtypeStruct((GROUP, WIDTH), BF16),
            jax.ShapeDtypeStruct((CORE_HID, WIDTH), BF16),
            jax.ShapeDtypeStruct((1, CORE_HID), F32),
            jax.ShapeDtypeStruct((CORE_HID, WIDTH), BF16),
        ),
        in_specs=[hbm] * 5,
        out_specs=(vmem,) * 4,
        scratch_shapes=[
            pltpu.VMEM((2, CHUNKS, GROUP, WIDE), BF16),
            pltpu.VMEM((PADDED, WIDE), BF16),
            pltpu.VMEM((PADDED, WIDE), BF16),
            pltpu.VMEM((HID,), F32),
            pltpu.VMEM((1, PADDED), F32),
            pltpu.VMEM((2, CHUNKS, GROUP, PADDED), BF16),
            pltpu.VMEM((2, CHUNKS, 2, EIGHTH, PADDED), BF16),
            pltpu.VMEM((2, CHUNKS, 2, QUARTER, PADDED), BF16),
            pltpu.VMEM((2, CHUNKS, 2, QUARTER, PADDED), BF16),
            pltpu.VMEM((2, CHUNKS, GROUP, PADDED), BF16),
            pltpu.VMEM((CHUNKS, QUARTER, PADDED), F32),
            pltpu.VMEM((CHUNKS, GROUP, WIDE), BF16),
            pltpu.VMEM((2, 4, GROUP, WIDE), BF16),
            pltpu.VMEM((GROUP, WIDE), BF16),
            pltpu.VMEM((2, 2, HALF, WIDTH), BF16),
            pltpu.VMEM((2, PADDED, WIDE), F32),
            pltpu.VMEM((2, 2, CORE_HID, WIDTH), BF16),
            pltpu.VMEM((2, 2, CORE_HID, WIDTH), BF16),
            pltpu.VMEM((2, CORE_HID, WIDTH), BF16),
            pltpu.VMEM((2, CORE_HID, WIDTH), BF16),
            pltpu.VMEM((8, PADDED), F32),
            pltpu.VMEM((8, PADDED), F32),
            pltpu.VMEM((8, PADDED), F32),
            pltpu.VMEM((8, PADDED), F32),
            pltpu.SemaphoreType.DMA((11,)),
            pltpu.SemaphoreType.DMA((360,)),
            pltpu.SemaphoreType.DMA((360,)),
        ],
        compiler_params=pltpu.CompilerParams(
            collective_id=0, has_side_effects=True, vmem_limit_bytes=58 << 20
        ),
        cost_estimate=pl.CostEstimate(
            flops=11_300_000_000, bytes_accessed=4_000_000, transcendentals=0
        ),
    )(tokens, out_grad, w_in.T, bias_in, w_out)
    ig, wgi, bg, wgo = pl.pallas_call(
        hand_over,
        name="hand_over",
        out_shape=tuple(jax.ShapeDtypeStruct(v.shape, v.dtype) for v in (ig, wgi, bg, wgo)),
        in_specs=[vmem] * 4,
        out_specs=(vmem,) * 4,
    )(ig, wgi, bg, wgo)
    return ig, wgi.T, bg.reshape(CORE_HID), wgo


def solution(mesh):
    in_specs = (
        P(("col", "rep"), "row"),
        P(("col", "rep"), "row"),
        P("row", "col"),
        P("col"),
        P("col", "row"),
    )
    out_specs = (
        P(("col", "rep"), "row"),
        P("row", ("col", "rep")),
        P(("col", "rep")),
        P(("col", "rep"), "row"),
    )
    return jax.shard_map(local, mesh=mesh, in_specs=in_specs, out_specs=out_specs, check_vma=False)
```

```python
import jax
import jax.numpy as jnp
from jax import lax
from jax.experimental import pallas as pl
from jax.experimental.pallas import tpu as pltpu
from jax.sharding import PartitionSpec as P

MESH = pl.DeviceIdType.MESH
BF16, F32 = jnp.bfloat16, jnp.float32
NX, NZ = 4, 8
GROUP, HALF = 128, 64
WIDTH, WIDE = 640, 1280
HID, CORE_HID = 864, 432
PADDED = 896
PARTS = ((0, 192), (192, 240))
PLACE = (0, 384)
LANES = ((0, 384), (384, 512), (0, 896))
QUARTER, EIGHTH = 32, 16
CHUNKS = 8
SCALE = 1.0 / 64.0
DIRECT = ((1, 0, 7), (1, 1, 7))
SCHEDULE = (
    ("sx",), ("zs", 0), ("wf", 0, 0), ("zf", 0, 1, 0), ("zf", 0, 2, 1), ("r1", 0, 0, 0), ("zf", 0, 1, 1),
    ("zf", 0, 2, 0), ("r1", 0, 0, 1), ("r1", 0, 0, 2), ("wf", 0, 1), ("r2", 0, 0, 0), ("zf", 0, 3, 0),
    ("zf", 0, 4, 1), ("r2", 0, 0, 1), ("r2", 0, 0, 2), ("r1", 0, 1, 0), ("r3", 0, 0, 0), ("r1", 0, 1, 1),
    ("r1", 0, 1, 2), ("zf", 0, 3, 1), ("r1", 0, 0, 4), ("zf", 0, 4, 0), ("r3", 0, 0, 1), ("r1", 0, 1, 3),
    ("r2", 0, 1, 0), ("r1", 0, 0, 3), ("r4", 0, 0, 0), ("r1", 0, 1, 4), ("wf", 1, 0), ("zf", 0, 5, 0),
    ("r2", 0, 1, 2), ("r2", 0, 0, 4), ("zf", 0, 6, 1), ("zs", 1), ("r4", 0, 0, 1), ("r2", 0, 1, 3),
    ("r3", 0, 0, 2), ("r2", 0, 1, 1), ("r3", 0, 1, 0), ("r2", 0, 0, 3), ("r5", 0, 0, 0), ("r2", 0, 1, 4),
    ("r3", 0, 1, 2), ("r3", 0, 0, 4), ("r5", 0, 0, 1), ("r3", 0, 1, 3), ("r4", 0, 0, 2), ("wf", 1, 1),
    ("r3", 0, 1, 1), ("r4", 0, 1, 0), ("r1", 0, 0, 7), ("r1", 0, 1, 7), ("r1", 1, 0, 0), ("r3", 0, 1, 4),
    ("r1", 0, 0, 6), ("r4", 0, 0, 4), ("zf", 1, 1, 0), ("zf", 1, 2, 1), ("r1", 0, 1, 6), ("r1", 0, 1, 5),
    ("r4", 0, 1, 1), ("r4", 0, 1, 2), ("r1", 0, 0, 5), ("r2", 0, 0, 7), ("r4", 0, 1, 3), ("r2", 0, 1, 7),
    ("r2", 1, 0, 0), ("r3", 0, 0, 3), ("zf", 1, 1, 1), ("r5", 0, 1, 0), ("r5", 0, 0, 2), ("r4", 0, 1, 4),
    ("zf", 1, 2, 0), ("r2", 0, 0, 6), ("r5", 0, 0, 4), ("r2", 0, 1, 6), ("r2", 0, 1, 5), ("r5", 0, 1, 1),
    ("wg", 1, 2, 0), ("zf", 1, 3, 0), ("r2", 0, 0, 5), ("zf", 1, 4, 1), ("r3", 0, 0, 7), ("r5", 0, 1, 3),
    ("r5", 0, 1, 2), ("r3", 0, 1, 7), ("r3", 1, 0, 0), ("r4", 0, 0, 3), ("r5", 0, 1, 4), ("r1", 1, 0, 1),
    ("zf", 1, 3, 1), ("r3", 0, 0, 6), ("r3", 0, 1, 6), ("zf", 1, 4, 0), ("r3", 0, 1, 5), ("r3", 0, 0, 5),
    ("r4", 0, 0, 7), ("r1", 1, 0, 4), ("r4", 0, 1, 7), ("r1", 1, 0, 2), ("r4", 1, 0, 0), ("zf", 1, 5, 0),
    ("r2", 1, 0, 1), ("zf", 1, 6, 1), ("r5", 0, 0, 3), ("wg", 1, 2, 1), ("r4", 0, 0, 6), ("r4", 0, 1, 6),
    ("r4", 0, 1, 5), ("r1", 1, 1, 4), ("r4", 0, 0, 5), ("r5", 0, 0, 7), ("r1", 1, 0, 3), ("r1", 1, 1, 6),
    ("r5", 1, 0, 0), ("r2", 1, 0, 4), ("r1", 1, 0, 6), ("r3", 1, 0, 1), ("r5", 0, 0, 6), ("r1", 1, 1, 5),
    ("r1", 1, 0, 5), ("r2", 1, 1, 4), ("r5", 0, 1, 7), ("r1", 1, 0, 7), ("r1", 1, 1, 7), ("r2", 1, 1, 6),
    ("r3", 1, 0, 4), ("r5", 0, 0, 5), ("r2", 1, 0, 6), ("r5", 0, 1, 6), ("r4", 1, 0, 1), ("wg", 1, 2, 3),
    ("r3", 1, 1, 4), ("r2", 1, 1, 5), ("r2", 1, 0, 5), ("r5", 0, 1, 5), ("wg", 1, 2, 2), ("cs", 1, 1),
    ("r1", 1, 1, 3), ("r3", 1, 1, 7), ("r3", 1, 1, 6), ("r3", 1, 0, 7), ("r4", 1, 0, 4), ("r2", 1, 0, 3),
    ("r2", 1, 0, 2), ("r3", 1, 0, 6), ("r5", 1, 0, 1), ("cs", 1, 0), ("wg", 0, 0, 0), ("fs", 1, 1),
    ("r4", 1, 1, 4), ("r3", 1, 1, 5), ("r3", 1, 0, 5), ("r2", 1, 1, 3), ("fs", 1, 0), ("r5", 1, 1, 7),
    ("r4", 1, 1, 6), ("r5", 1, 0, 7), ("ip", 7), ("ss", 0, 0, 0), ("r5", 1, 0, 4), ("ss", 1, 0, 1),
    ("r3", 1, 0, 3), ("r1", 1, 1, 0), ("r1", 1, 1, 1), ("r4", 1, 0, 6), ("r5", 1, 1, 4), ("ip", 4),
    ("r4", 1, 1, 5), ("r1", 1, 1, 2), ("r4", 1, 0, 5), ("bp", 7), ("r3", 1, 0, 2), ("r3", 1, 1, 3),
    ("wo", 1, 1), ("r5", 1, 1, 6), ("wg", 0, 1, 3), ("r2", 1, 1, 0), ("r4", 1, 0, 3), ("r2", 1, 1, 1),
    ("r5", 1, 0, 6), ("ip", 6), ("r5", 1, 1, 5), ("ss", 0, 1, 1), ("r2", 1, 1, 2), ("ss", 0, 1, 0),
    ("r5", 1, 0, 5), ("ip", 5), ("r4", 1, 0, 2), ("ss", 1, 1, 0), ("ss", 1, 1, 1), ("r4", 1, 1, 3),
    ("bp", 5), ("wg", 0, 1, 2), ("r3", 1, 1, 0), ("r5", 1, 0, 3), ("wo", 1, 0), ("wg", 0, 0, 3),
    ("r3", 1, 1, 2), ("bp", 6), ("r3", 1, 1, 1), ("wg", 0, 0, 2), ("r5", 1, 1, 3), ("ip", 3), ("bp", 4),
    ("bp", 3), ("ss", 0, 2, 1), ("r4", 1, 1, 0), ("r5", 1, 0, 2), ("wg", 0, 0, 1), ("cs", 0, 0),
    ("ss", 1, 2, 0), ("r4", 1, 1, 2), ("r4", 1, 1, 1), ("r5", 1, 1, 0), ("ss", 0, 2, 0), ("ip", 0),
    ("bp", 0), ("fs", 0, 0), ("r5", 1, 1, 2), ("ss", 1, 2, 1), ("ip", 2), ("r5", 1, 1, 1), ("ip", 1),
    ("bp", 2), ("wg", 0, 1, 0), ("ss", 0, 3, 1), ("bp", 1), ("bc",), ("wg", 0, 1, 1), ("cs", 0, 1),
    ("ss", 1, 3, 0), ("ss", 0, 3, 0), ("bf",), ("ss", 1, 3, 1), ("fs", 0, 1), ("wo", 0, 0), ("bo",), ("yb",),
    ("wo", 0, 1), ("io",),
)


def contract(a, b, dim_a, dim_b):
    return lax.dot_general(
        a, b, (((dim_a,), (dim_b,)), ((), ())), preferred_element_type=F32
    )


def bend_of(value):
    return jnp.tanh(0.7978845608 * (value + 0.044715 * value * value * value))


def kernel(
    tok, og, win, bias, wout,
    ig_out, wgi_out, bg_out, wgo_out,
    xg, wi, wo, bias_raw, bias_v, part, first, second_out, second, across, ap, pre,
    ig, zr, ys, yr, wg, core_out, core_in, far_out, far_in,
    bsum, bcore, bpair, bfar,
    local_sem, send_sem, recv_sem,
):
    row, col, rep = lax.axis_index("row"), lax.axis_index("col"), lax.axis_index("rep")
    yh, x = row // NX, row % NX
    yl, z = col // NZ, col % NZ

    def at(yh_=yh, x_=x, yl_=yl, z_=z, rep_=rep):
        return {"row": yh_ * NX + x_, "col": yl_ * NZ + z_, "rep": rep_}

    x_right, x_left = at(x_=(x + 1) % NX), at(x_=(x + 3) % NX)
    x_across = at(x_=(x + 2) % NX)
    z_right, z_left = at(z_=(z + 1) % NZ), at(z_=(z + 7) % NZ)
    core = at(rep_=1 - rep)
    y_far = at(yh_=1 - yh)
    y_peers = [
        (yh, 1 - yl, at(yl_=1 - yl)),
        (1 - yh, yl, y_far),
        (1 - yh, 1 - yl, at(yh_=1 - yh, yl_=1 - yl)),
    ]

    counts = {"local": 0, "remote": 0}
    sent, arrived = [], set()

    def move(src, dst):
        copy = pltpu.make_async_copy(src, dst, local_sem.at[counts["local"]])
        counts["local"] += 1
        copy.start()
        return copy

    def send(src, dst, device):
        number = counts["remote"]
        counts["remote"] += 1
        copy = pltpu.make_async_remote_copy(
            src_ref=src,
            dst_ref=dst,
            send_sem=send_sem.at[number],
            recv_sem=recv_sem.at[number],
            device_id=device,
            device_id_type=MESH,
        )
        copy.start()
        sent.append(copy)
        return copy

    def need(*copies):
        for copy in copies:
            if id(copy) not in arrived:
                arrived.add(id(copy))
                copy.wait_recv()

    def span(start, size, unit):
        return pl.ds(pl.multiple_of(start, unit), size)

    my_rows = span(yl * HALF, HALF, HALF)
    my_lanes = span(yh * WIDTH, WIDTH, 128)
    far_lanes = span((1 - yh) * WIDTH, WIDTH, 128)

    def source_rows(which, of):
        start, size = PARTS[of]
        return span(which * CORE_HID + start, size, 16)

    def held_rows(which, of):
        size = PARTS[of][1]
        return span(PLACE[of] + which * size, size, 16)

    own = {}
    for j, (block, weights, held) in enumerate(((tok, win, wi), (og, wout, wo))):
        own[j] = [
            move(block.at[span(yh * HALF, HALF, HALF)], xg.at[j, 0, my_rows, my_lanes])
        ]
        for of in (0, 1):
            own[j, of] = [
                move(
                    weights.at[pl.ds(which * CORE_HID + PARTS[of][0], PARTS[of][1])],
                    held.at[
                        pl.ds(PLACE[of] + which * PARTS[of][1], PARTS[of][1]), my_lanes
                    ],
                )
                for which in (0, 1)
            ]
    own_bias = [move(bias, bias_raw)]

    def own_ready(key):
        while own[key]:
            own[key].pop().wait()

    own["bias"] = own_bias

    def bias_ready():
        if not own["bias"]:
            return
        own_ready("bias")
        raw = bias_raw[...].reshape(1, HID)
        blocks = [
            raw[:, which * CORE_HID + start : which * CORE_HID + start + size]
            for start, size in PARTS
            for which in (0, 1)
        ]
        blocks.append(jnp.zeros((1, PADDED - HID), F32))
        bias_v[...] = jnp.concatenate(blocks, axis=1)

    for held in (wi, wo):
        held[pl.ds(HID, PADDED - HID)] = jnp.zeros((PADDED - HID, WIDE), BF16)

    barrier = pltpu.get_barrier_semaphore()
    everyone = [x_right, x_left, x_across, z_right, z_left, core] + [p[2] for p in y_peers]
    for device in everyone:
        pl.semaphore_signal(barrier, inc=1, device_id=device, device_id_type=MESH)
    pl.semaphore_wait(barrier, len(everyone))

    spread, weight_far, weight_core, ring = {}, {}, {}, {}
    halves = (pl.ds(0, HALF), pl.ds(HALF, HALF))

    def send_block(j):
        source = og if j else tok
        spread[j] = [
            send(
                source.at[span(to_yh * HALF, HALF, HALF)],
                xg.at[j, 0, my_rows, my_lanes],
                device,
            )
            for to_yh, _, device in y_peers
        ]

    def send_weights(j, of):
        source, held = (wout, wo) if j else (win, wi)
        weight_far[j, of] = send(
            source.at[source_rows(rep, of)], held.at[held_rows(rep, of), my_lanes], y_far
        )

    def begin():
        send_block(0)
        send_weights(0, 0)

    def ring_send(j, source, slot, half, device):
        rows = halves[half]
        ring[j, slot, half] = send(xg.at[j, source, rows], xg.at[j, slot, rows], device)

    def ring_start(j):
        own_ready(j)
        need(*spread[j])
        for half in (0, 1):
            ring_send(j, 0, 1, half, z_right)
            ring_send(j, 0, 2, 1 - half, z_left)
        if j == 0:
            send_weights(0, 1)

    def ring_pass(j, slot, half):
        need(ring[j, slot, half])
        ring_send(j, slot, min(slot + 2, 7), half, z_right if slot % 2 else z_left)

    def chunk_ready(j, slot):
        if slot == 0:
            own_ready(j)
            need(*spread[j])
        else:
            need(ring[j, slot, 0], ring[j, slot, 1])

    def weights_pass(j, of):
        need(weight_far[j, of])
        block = (wo if j else wi).at[held_rows(rep, of), far_lanes]
        weight_core[j, of] = send(block, block, core)
        if (j, of) == (0, 0):
            send_block(1)
        if (j, of) == (0, 1):
            send_weights(1, 0)
            send_weights(1, 1)

    def weights_ready(j, lanes):
        for of in (0, 1):
            if lanes in (of, 2):
                own_ready((j, of))
                need(weight_core[j, of])

    stage = {}

    def quarter(of, offset=0, size=QUARTER):
        return span(((x + of) % NX) * QUARTER + offset, size, EIGHTH)

    low16, high16 = pl.ds(0, EIGHTH), pl.ds(EIGHTH, EIGHTH)

    def multiply(j, lanes, slot):
        chunk_ready(j, slot)
        weights_ready(j, lanes)
        at_lanes = pl.ds(*LANES[lanes])
        weights = (wo if j else wi)[at_lanes]
        part[j, slot, :, at_lanes] = contract(xg[j, slot], weights, 1, 1).astype(BF16)
        if (j, lanes, slot) in DIRECT:
            stage[2, j, lanes, slot] = [
                send(part.at[j, slot, quarter(of), at_lanes], target, device)
                for of, target, device in (
                    (2, across.at[j, slot, :, at_lanes], x_across),
                    (1, second.at[j, slot, 0, :, at_lanes], x_right),
                    (3, second.at[j, slot, 1, :, at_lanes], x_left),
                )
            ]
            return
        rows = (quarter(2, 0, EIGHTH), quarter(2, EIGHTH, EIGHTH))
        stage[1, j, lanes, slot] = [
            send(
                part.at[j, slot, rows[side], at_lanes],
                first.at[j, slot, side, :, at_lanes],
                x_left if side else x_right,
            )
            for side in (0, 1)
        ]

    def add_first(j, lanes, slot):
        at_lanes = pl.ds(*LANES[lanes])
        copies = []
        for side in (0, 1):
            need(stage[1, j, lanes, slot][side])
            of = 3 if side else 1
            summed = (high16, EIGHTH) if side else (low16, 0)
            plain = (low16, 0) if side else (high16, EIGHTH)
            second_out[j, slot, side, summed[0], at_lanes] = (
                part[j, slot, quarter(of, summed[1], EIGHTH), at_lanes].astype(F32)
                + first[j, slot, side, :, at_lanes].astype(F32)
            ).astype(BF16)
            second_out[j, slot, side, plain[0], at_lanes] = part[
                j, slot, quarter(of, plain[1], EIGHTH), at_lanes
            ]
            copies.append(
                send(
                    second_out.at[j, slot, side, :, at_lanes],
                    second.at[j, slot, side, :, at_lanes],
                    x_left if side else x_right,
                )
            )
        stage[2, j, lanes, slot] = copies

    def activate(j, lanes, slot):
        need(*stage[2, j, lanes, slot])
        at_lanes = pl.ds(*LANES[lanes])
        mine = quarter(0)
        total = (
            part[j, slot, mine, at_lanes].astype(F32)
            + second[j, slot, 0, :, at_lanes].astype(F32)
            + second[j, slot, 1, :, at_lanes].astype(F32)
        )
        direct = (j, lanes, slot) in DIRECT
        if direct:
            total = total + across[j, slot, :, at_lanes].astype(F32)
        if j == 0:
            bias_ready()
            value = total + bias_v[:, at_lanes]
            pre[slot, :, at_lanes] = value
            result = 0.5 * value * (1.0 + bend_of(value))
        else:
            value = pre[slot, :, at_lanes]
            bend = bend_of(value)
            slope = 0.7978845608 * (1.0 + 3.0 * 0.044715 * value * value)
            result = total * (
                0.5 * (1.0 + bend) + 0.5 * value * (1.0 - bend * bend) * slope
            )
        ap[j, slot, mine, at_lanes] = result.astype(BF16)
        block = ap.at[j, slot, mine, at_lanes]
        others = [x_across] * direct + [x_right, x_left]
        stage[4 if direct else 3, j, lanes, slot] = [
            send(block, block, device) for device in others
        ]

    def hand_on(j, lanes, slot):
        at_lanes = pl.ds(*LANES[lanes])
        copies = []
        for side in (0, 1):
            need(stage[3, j, lanes, slot][side])
            rows = quarter(1, EIGHTH, EIGHTH) if side else quarter(3, 0, EIGHTH)
            block = ap.at[j, slot, rows, at_lanes]
            copies.append(send(block, block, x_left if side else x_right))
        stage[4, j, lanes, slot] = copies

    def all_here(j, lanes, slot):
        need(*stage[4, j, lanes, slot])

    core_copy, far_copy = {}, {}
    started = set()

    def weight_grad(j, lanes, pair):
        for slot in (2 * pair, 2 * pair + 1):
            chunk_ready(j, slot)
        slots, hidden = pl.ds(2 * pair, 2), pl.ds(*LANES[lanes])
        left = ap[1 - j, slots, :, hidden].reshape(2 * GROUP, LANES[lanes][1])
        right = xg[j, slots].reshape(2 * GROUP, WIDE)
        product = contract(left, right, 0, 0)
        wg[j, hidden] = wg[j, hidden] + product if (j, lanes) in started else product
        started.add((j, lanes))

    def core_send(j, of):
        rows = pl.ds(*PARTS[of])
        for far, lanes in ((1, far_lanes), (0, my_lanes)):
            block = wg[j, held_rows(1 - rep, of), lanes] * SCALE
            core_out[j, far, rows] = block.astype(BF16)
            core_copy[j, of, far] = send(
                core_out.at[j, far, rows], core_in.at[j, far, rows], core
            )

    def far_send(j, of):
        need(core_copy[j, of, 1])
        rows = pl.ds(*PARTS[of])
        block = wg[j, held_rows(rep, of), far_lanes] * SCALE
        far_out[j, rows] = (block + core_in[j, 1, rows].astype(F32)).astype(BF16)
        far_copy[j, of] = send(far_out.at[j, rows], far_in.at[j, rows], y_far)

    def weight_out(j, of):
        need(core_copy[j, of, 0], far_copy[j, of])
        rows = pl.ds(*PARTS[of])
        block = wg[j, held_rows(rep, of), my_lanes] * SCALE
        total = block + core_in[j, 0, rows].astype(F32)
        out = wgo_out if j else wgi_out
        out[rows] = (total + far_in[j, rows].astype(F32)).astype(BF16)

    bias_copy = {}

    def bias_part(slot):
        rows = ap[1, slot].astype(F32).reshape(GROUP // 8, 8, PADDED).sum(axis=0)
        bsum[...] = bsum[...] + rows if "bias" in started else rows
        started.add("bias")

    def bias_core():
        bias_copy[0] = send(bsum, bcore, core)

    def bias_far():
        need(bias_copy[0])
        bpair[...] = bsum[...] + bcore[...]
        bias_copy[1] = send(bpair, bfar, y_far)

    def bias_out():
        need(bias_copy[1])
        total = jnp.sum(bpair[...] + bfar[...], axis=0, keepdims=True) * SCALE
        mine = [
            jnp.concatenate(
                [
                    total[:, PLACE[of] + which * size : PLACE[of] + (which + 1) * size]
                    for of, (_, size) in enumerate(PARTS)
                ],
                axis=1,
            )
            for which in (0, 1)
        ]
        bg_out[...] = jnp.where(rep == 0, mine[0], mine[1])

    ring_sum, back = {}, []

    def input_part(slot):
        ig[slot] = contract(ap[1, slot], wi[...], 1, 0).astype(BF16)

    def sum_pass(side, step, half):
        slot = ((7, 6, 4, 2), (7, 5, 3, 1))[side][step]
        rows = halves[half]
        if (side, step - 1, half) in ring_sum:
            need(ring_sum[side, step - 1, half])
            ig[slot, rows] = (
                ig[slot, rows].astype(F32) + zr[side, step - 1, rows].astype(F32)
            ).astype(BF16)
        ring_sum[side, step, half] = send(
            ig.at[slot, rows], zr.at[side, step, rows], z_left if side else z_right
        )

    def sum_end():
        for half, rows in enumerate(halves):
            need(ring_sum[0, 3, half], ring_sum[1, 3, half])
            ys[rows] = (
                ig[0, rows].astype(F32)
                + zr[0, 3, rows].astype(F32)
                + zr[1, 3, rows].astype(F32)
            ).astype(BF16)
        for to_yh, to_yl, device in y_peers:
            lanes = span(to_yh * WIDTH, WIDTH, 128)
            block = ys.at[span(to_yl * HALF, HALF, HALF), lanes]
            back.append(send(block, yr.at[yh, yl], device))
        yr[yh, yl] = ys[my_rows, my_lanes]

    def input_out():
        need(*back)
        for half, rows in enumerate(halves):
            total = yr[half, 0].astype(F32) + yr[half, 1].astype(F32)
            ig_out[rows] = total.astype(BF16)

    steps = {
        "sx": begin, "zs": ring_start, "zf": ring_pass, "wf": weights_pass,
        "r1": multiply, "r2": add_first, "r3": activate, "r4": hand_on, "r5": all_here,
        "wg": weight_grad, "cs": core_send, "fs": far_send, "wo": weight_out,
        "bp": bias_part, "bc": bias_core, "bf": bias_far, "bo": bias_out,
        "ip": input_part, "ss": sum_pass, "yb": sum_end, "io": input_out,
    }
    for name, *which in SCHEDULE:
        steps[name](*which)
    for copy in sent:
        copy.wait_send()


def hand_over(*refs):
    copies = [
        pltpu.make_async_copy(refs[n], refs[4 + n], refs[8].at[n]) for n in range(4)
    ]
    for copy in copies:
        copy.start()
    for copy in copies:
        copy.wait()


def local(tokens, out_grad, w_in, bias_in, w_out):
    hbm, vmem = pl.BlockSpec(memory_space=pl.ANY), pl.BlockSpec(memory_space=pltpu.VMEM)
    ig, wgi, bg, wgo = pl.pallas_call(
        kernel,
        name="ffn_backward",
        out_shape=(
            pltpu.VMEM((GROUP, WIDTH), BF16),
            pltpu.VMEM((CORE_HID, WIDTH), BF16),
            pltpu.VMEM((1, CORE_HID), F32),
            pltpu.VMEM((CORE_HID, WIDTH), BF16),
        ),
        in_specs=[hbm] * 5,
        out_specs=(vmem,) * 4,
        scratch_shapes=[
            pltpu.VMEM((2, CHUNKS, GROUP, WIDE), BF16),
            pltpu.VMEM((PADDED, WIDE), BF16),
            pltpu.VMEM((PADDED, WIDE), BF16),
            pltpu.VMEM((HID,), F32),
            pltpu.VMEM((1, PADDED), F32),
            pltpu.VMEM((2, CHUNKS, GROUP, PADDED), BF16),
            pltpu.VMEM((2, CHUNKS, 2, EIGHTH, PADDED), BF16),
            pltpu.VMEM((2, CHUNKS, 2, QUARTER, PADDED), BF16),
            pltpu.VMEM((2, CHUNKS, 2, QUARTER, PADDED), BF16),
            pltpu.VMEM((2, CHUNKS, QUARTER, PADDED), BF16),
            pltpu.VMEM((2, CHUNKS, GROUP, PADDED), BF16),
            pltpu.VMEM((CHUNKS, QUARTER, PADDED), F32),
            pltpu.VMEM((CHUNKS, GROUP, WIDE), BF16),
            pltpu.VMEM((2, 4, GROUP, WIDE), BF16),
            pltpu.VMEM((GROUP, WIDE), BF16),
            pltpu.VMEM((2, 2, HALF, WIDTH), BF16),
            pltpu.VMEM((2, PADDED, WIDE), F32),
            pltpu.VMEM((2, 2, CORE_HID, WIDTH), BF16),
            pltpu.VMEM((2, 2, CORE_HID, WIDTH), BF16),
            pltpu.VMEM((2, CORE_HID, WIDTH), BF16),
            pltpu.VMEM((2, CORE_HID, WIDTH), BF16),
            pltpu.VMEM((8, PADDED), F32),
            pltpu.VMEM((8, PADDED), F32),
            pltpu.VMEM((8, PADDED), F32),
            pltpu.VMEM((8, PADDED), F32),
            pltpu.SemaphoreType.DMA((11,)),
            pltpu.SemaphoreType.DMA((360,)),
            pltpu.SemaphoreType.DMA((360,)),
        ],
        compiler_params=pltpu.CompilerParams(
            collective_id=0, has_side_effects=True, vmem_limit_bytes=58 << 20
        ),
        cost_estimate=pl.CostEstimate(
            flops=11_300_000_000, bytes_accessed=4_000_000, transcendentals=0
        ),
    )(tokens, out_grad, w_in.T, bias_in, w_out)
    ig, wgi, bg, wgo = pl.pallas_call(
        hand_over,
        name="hand_over",
        out_shape=tuple(jax.ShapeDtypeStruct(v.shape, v.dtype) for v in (ig, wgi, bg, wgo)),
        in_specs=[vmem] * 4,
        out_specs=(hbm,) * 4,
        scratch_shapes=[pltpu.SemaphoreType.DMA((4,))],
    )(*(pltpu.with_memory_space_constraint(v, pltpu.VMEM) for v in (ig, wgi, bg, wgo)))
    return ig, wgi.T, bg.reshape(CORE_HID), wgo


def solution(mesh):
    in_specs = (
        P(("col", "rep"), "row"),
        P(("col", "rep"), "row"),
        P("row", "col"),
        P("col"),
        P("col", "row"),
    )
    out_specs = (
        P(("col", "rep"), "row"),
        P("row", ("col", "rep")),
        P(("col", "rep")),
        P(("col", "rep"), "row"),
    )
    return jax.shard_map(local, mesh=mesh, in_specs=in_specs, out_specs=out_specs, check_vma=False)
```

```python
import jax
import jax.numpy as jnp
from jax import lax
from jax.experimental import pallas as pl
from jax.experimental.pallas import tpu as pltpu
from jax.sharding import PartitionSpec as P

MESH = pl.DeviceIdType.MESH
BF16, F32 = jnp.bfloat16, jnp.float32
NX, NZ = 4, 8
GROUP, HALF = 128, 64
WIDTH, WIDE = 640, 1280
HID, CORE_HID = 864, 432
PADDED = 896
PARTS = ((0, 192), (192, 240))
PLACE = (0, 384)
LANES = ((0, 384), (384, 512), (0, 896))
QUARTER, EIGHTH = 32, 16
CHUNKS = 8
SCALE = 1.0 / 64.0
DIRECT = ((1, 0, 7), (1, 1, 7))
SCHEDULE = (
    ("sx",), ("zs", 0), ("wf", 0, 0), ("zf", 0, 1, 0), ("zf", 0, 2, 1), ("r1", 0, 0, 0), ("r1", 0, 0, 1),
    ("zf", 0, 2, 0), ("zf", 0, 1, 1), ("r1", 0, 0, 2), ("r2", 0, 0, 0), ("wf", 0, 1), ("zf", 0, 3, 0),
    ("zf", 0, 4, 1), ("r2", 0, 0, 1), ("r2", 0, 0, 2), ("r1", 0, 1, 0), ("r3", 0, 0, 0), ("ra", 0, 0, 0),
    ("r1", 0, 1, 1), ("r1", 0, 1, 2), ("r1", 0, 0, 3), ("r3", 0, 0, 1), ("ra", 0, 0, 1), ("zf", 0, 4, 0),
    ("zf", 0, 3, 1), ("r3", 0, 0, 2), ("ra", 0, 0, 2), ("r1", 0, 1, 3), ("r2", 0, 1, 0), ("r4", 0, 0, 0),
    ("r1", 0, 0, 4), ("r2", 0, 1, 1), ("r2", 0, 1, 2), ("zf", 0, 5, 0), ("zf", 0, 6, 1), ("r2", 0, 0, 3),
    ("zs", 1), ("r4", 0, 0, 1), ("wf", 1, 0), ("r4", 0, 0, 2), ("r1", 0, 1, 4), ("r2", 0, 1, 3),
    ("r3", 0, 1, 0), ("ra", 0, 1, 0), ("r5", 0, 0, 0), ("r2", 0, 0, 4), ("r1", 0, 1, 5), ("r1", 1, 0, 0),
    ("r1", 0, 0, 6), ("r3", 0, 0, 3), ("r5", 0, 0, 1), ("ra", 0, 0, 3), ("r1", 0, 0, 5), ("r5", 0, 0, 2),
    ("r2", 0, 1, 4), ("r1", 0, 1, 6), ("wf", 1, 1), ("r1", 0, 0, 7), ("r4", 0, 1, 0), ("r1", 0, 1, 7),
    ("r3", 0, 0, 4), ("r2", 0, 1, 5), ("ra", 0, 0, 4), ("r2", 1, 0, 0), ("r2", 0, 0, 6), ("r3", 0, 1, 3),
    ("r3", 0, 1, 2), ("r3", 0, 1, 1), ("r4", 0, 0, 3), ("r2", 0, 0, 5), ("zf", 1, 1, 0), ("zf", 1, 2, 1),
    ("r3", 0, 1, 4), ("ra", 0, 1, 3), ("r2", 0, 1, 6), ("r2", 0, 0, 7), ("r5", 0, 1, 0), ("r2", 0, 1, 7),
    ("r3", 0, 1, 5), ("r4", 0, 0, 4), ("zf", 1, 1, 1), ("zf", 1, 2, 0), ("r3", 1, 0, 0), ("r3", 0, 0, 6),
    ("ra", 0, 0, 6), ("r5", 0, 0, 3), ("ra", 0, 1, 1), ("r3", 0, 0, 5), ("ra", 0, 0, 5), ("r4", 0, 1, 3),
    ("r1", 1, 0, 1), ("zf", 1, 4, 1), ("r3", 0, 1, 6), ("ra", 0, 1, 6), ("zf", 1, 3, 0), ("r3", 0, 0, 7),
    ("ra", 0, 0, 7), ("r3", 0, 1, 7), ("ra", 0, 1, 2), ("r5", 0, 0, 4), ("r4", 1, 0, 0), ("ra", 0, 1, 4),
    ("r4", 0, 0, 6), ("r4", 0, 1, 1), ("zf", 1, 3, 1), ("zf", 1, 4, 0), ("r1", 1, 0, 4), ("r5", 0, 1, 3),
    ("r1", 1, 0, 3), ("r2", 1, 0, 1), ("r1", 1, 1, 4), ("ra", 0, 1, 5), ("r4", 0, 0, 7), ("r4", 0, 1, 6),
    ("r4", 0, 0, 5), ("r4", 0, 1, 2), ("r5", 1, 0, 0), ("zf", 1, 5, 0), ("zf", 1, 6, 1), ("ra", 0, 1, 7),
    ("r4", 0, 1, 4), ("r5", 0, 0, 6), ("r5", 0, 1, 1), ("wg", 1, 2, 0), ("r3", 1, 0, 1), ("r2", 1, 0, 4),
    ("r1", 1, 1, 3), ("r1", 1, 1, 5), ("r5", 0, 0, 7), ("r5", 0, 1, 6), ("r1", 1, 0, 6), ("r4", 0, 1, 5),
    ("r5", 0, 0, 5), ("r1", 1, 1, 6), ("r4", 0, 1, 7), ("r1", 1, 0, 5), ("r5", 0, 1, 4), ("r1", 1, 0, 2),
    ("r4", 1, 0, 1), ("r1", 1, 0, 7), ("r1", 1, 1, 7), ("r2", 1, 1, 5), ("r2", 1, 0, 6), ("r5", 0, 1, 5),
    ("wg", 1, 2, 2), ("r2", 1, 1, 6), ("r2", 1, 0, 5), ("r5", 0, 1, 7), ("wg", 1, 2, 3), ("r3", 1, 0, 7),
    ("r5", 1, 0, 1), ("wg", 0, 0, 0), ("r3", 1, 1, 7), ("r5", 0, 1, 2), ("wg", 1, 2, 1), ("r3", 1, 0, 6),
    ("r3", 1, 1, 6), ("cs", 1, 1), ("r3", 1, 1, 5), ("r3", 1, 0, 5), ("cs", 1, 0), ("r3", 1, 0, 4),
    ("r5", 1, 0, 7), ("r2", 1, 1, 4), ("r2", 1, 0, 3), ("r2", 1, 1, 3), ("r2", 1, 0, 2), ("fs", 1, 1),
    ("r5", 1, 1, 7), ("ip", 7), ("ss", 0, 0, 0), ("r4", 1, 0, 6), ("fs", 1, 0), ("ss", 1, 0, 1),
    ("r4", 1, 1, 6), ("bp", 7), ("r1", 1, 1, 2), ("r4", 1, 0, 5), ("r4", 1, 1, 5), ("r1", 1, 1, 1),
    ("r1", 1, 1, 0), ("r3", 1, 1, 4), ("r3", 1, 0, 3), ("r4", 1, 0, 4), ("r3", 1, 1, 3), ("r3", 1, 0, 2),
    ("r5", 1, 0, 6), ("wg", 0, 0, 3), ("r5", 1, 1, 6), ("ip", 6), ("ss", 0, 1, 1), ("r5", 1, 0, 5),
    ("r2", 1, 1, 2), ("r5", 1, 1, 5), ("ip", 5), ("ss", 1, 1, 0), ("ss", 1, 1, 1), ("r2", 1, 1, 1),
    ("r4", 1, 1, 4), ("wg", 0, 1, 3), ("r4", 1, 0, 3), ("bp", 5), ("wo", 1, 1), ("bp", 6), ("r4", 1, 1, 3),
    ("r2", 1, 1, 0), ("r5", 1, 0, 4), ("ss", 0, 1, 0), ("r4", 1, 0, 2), ("wg", 0, 0, 2), ("r3", 1, 1, 2),
    ("r3", 1, 1, 1), ("r5", 1, 1, 4), ("ip", 4), ("ss", 0, 2, 1), ("bp", 4), ("r5", 1, 1, 3),
    ("r5", 1, 0, 3), ("ip", 3), ("ss", 1, 2, 0), ("r3", 1, 1, 0), ("r5", 1, 0, 2), ("wg", 0, 0, 1),
    ("r4", 1, 1, 2), ("bp", 3), ("cs", 0, 0), ("wo", 1, 0), ("r4", 1, 1, 1), ("wg", 0, 1, 2),
    ("ss", 0, 2, 0), ("ss", 1, 2, 1), ("fs", 0, 0), ("r4", 1, 1, 0), ("r5", 1, 1, 2), ("ip", 2), ("bp", 2),
    ("wg", 0, 1, 1), ("ss", 0, 3, 1), ("r5", 1, 1, 1), ("ip", 1), ("bp", 1), ("ss", 1, 3, 0),
    ("r5", 1, 1, 0), ("bp", 0), ("bc",), ("wg", 0, 1, 0), ("cs", 0, 1), ("ip", 0), ("bf",), ("ss", 0, 3, 0),
    ("ss", 1, 3, 1), ("fs", 0, 1), ("wo", 0, 0), ("bo",), ("yb",), ("wo", 0, 1), ("io",),
)


def contract(a, b, dim_a, dim_b):
    return lax.dot_general(
        a, b, (((dim_a,), (dim_b,)), ((), ())), preferred_element_type=F32
    )


def bend_of(value):
    return jnp.tanh(0.7978845608 * (value + 0.044715 * value * value * value))


def kernel(
    tok, og, win, bias, wout,
    ig_out, wgi_out, bg_out, wgo_out,
    xg, wi, wo, bias_raw, bias_v, part, first, second_out, second, across, ap, pre,
    ig, zr, ys, yr, wg, core_out, core_in, far_out, far_in,
    bsum, bcore, bpair, bfar,
    local_sem, send_sem, recv_sem,
):
    row, col, rep = lax.axis_index("row"), lax.axis_index("col"), lax.axis_index("rep")
    yh, x = row // NX, row % NX
    yl, z = col // NZ, col % NZ

    def at(yh_=yh, x_=x, yl_=yl, z_=z, rep_=rep):
        return {"row": yh_ * NX + x_, "col": yl_ * NZ + z_, "rep": rep_}

    x_right, x_left = at(x_=(x + 1) % NX), at(x_=(x + 3) % NX)
    x_across = at(x_=(x + 2) % NX)
    z_right, z_left = at(z_=(z + 1) % NZ), at(z_=(z + 7) % NZ)
    core = at(rep_=1 - rep)
    y_far = at(yh_=1 - yh)
    y_peers = [
        (yh, 1 - yl, at(yl_=1 - yl)),
        (1 - yh, yl, y_far),
        (1 - yh, 1 - yl, at(yh_=1 - yh, yl_=1 - yl)),
    ]

    counts = {"local": 0, "remote": 0}
    sent, arrived = [], set()

    def move(src, dst):
        copy = pltpu.make_async_copy(src, dst, local_sem.at[counts["local"]])
        counts["local"] += 1
        copy.start()
        return copy

    def send(src, dst, device):
        number = counts["remote"]
        counts["remote"] += 1
        copy = pltpu.make_async_remote_copy(
            src_ref=src,
            dst_ref=dst,
            send_sem=send_sem.at[number],
            recv_sem=recv_sem.at[number],
            device_id=device,
            device_id_type=MESH,
        )
        copy.start()
        sent.append(copy)
        return copy

    def need(*copies):
        for copy in copies:
            if id(copy) not in arrived:
                arrived.add(id(copy))
                copy.wait_recv()

    def span(start, size, unit):
        return pl.ds(pl.multiple_of(start, unit), size)

    my_rows = span(yl * HALF, HALF, HALF)
    my_lanes = span(yh * WIDTH, WIDTH, 128)
    far_lanes = span((1 - yh) * WIDTH, WIDTH, 128)

    def source_rows(which, of):
        start, size = PARTS[of]
        return span(which * CORE_HID + start, size, 16)

    def held_rows(which, of):
        size = PARTS[of][1]
        return span(PLACE[of] + which * size, size, 16)

    barrier = pltpu.get_barrier_semaphore()
    everyone = [x_right, x_left, x_across, z_right, z_left, core] + [p[2] for p in y_peers]
    for device in everyone:
        pl.semaphore_signal(barrier, inc=1, device_id=device, device_id_type=MESH)

    own = {}
    for j, (block, weights, held) in enumerate(((tok, win, wi), (og, wout, wo))):
        own[j] = [
            move(block.at[span(yh * HALF, HALF, HALF)], xg.at[j, 0, my_rows, my_lanes])
        ]
        for of in (0, 1):
            own[j, of] = [
                move(
                    weights.at[pl.ds(which * CORE_HID + PARTS[of][0], PARTS[of][1])],
                    held.at[
                        pl.ds(PLACE[of] + which * PARTS[of][1], PARTS[of][1]), my_lanes
                    ],
                )
                for which in (0, 1)
            ]
    own_bias = [move(bias, bias_raw)]

    def own_ready(key):
        while own[key]:
            own[key].pop().wait()

    own["bias"] = own_bias

    def bias_ready():
        if not own["bias"]:
            return
        own_ready("bias")
        raw = bias_raw[...].reshape(1, HID)
        blocks = [
            raw[:, which * CORE_HID + start : which * CORE_HID + start + size]
            for start, size in PARTS
            for which in (0, 1)
        ]
        blocks.append(jnp.zeros((1, PADDED - HID), F32))
        bias_v[...] = jnp.concatenate(blocks, axis=1)

    for held in (wi, wo):
        held[pl.ds(HID, PADDED - HID)] = jnp.zeros((PADDED - HID, WIDE), BF16)

    pl.semaphore_wait(barrier, len(everyone))

    spread, weight_far, weight_core, ring = {}, {}, {}, {}
    halves = (pl.ds(0, HALF), pl.ds(HALF, HALF))

    def send_block(j):
        source = og if j else tok
        spread[j] = [
            send(
                source.at[span(to_yh * HALF, HALF, HALF)],
                xg.at[j, 0, my_rows, my_lanes],
                device,
            )
            for to_yh, _, device in y_peers
        ]

    def send_weights(j, of):
        source, held = (wout, wo) if j else (win, wi)
        weight_far[j, of] = send(
            source.at[source_rows(rep, of)], held.at[held_rows(rep, of), my_lanes], y_far
        )

    def begin():
        send_block(0)
        send_weights(0, 0)

    def ring_send(j, source, slot, half, device):
        rows = halves[half]
        ring[j, slot, half] = send(xg.at[j, source, rows], xg.at[j, slot, rows], device)

    def ring_start(j):
        own_ready(j)
        need(*spread[j])
        for half in (0, 1):
            ring_send(j, 0, 1, half, z_right)
            ring_send(j, 0, 2, 1 - half, z_left)
        if j == 0:
            send_weights(0, 1)

    def ring_pass(j, slot, half):
        need(ring[j, slot, half])
        ring_send(j, slot, min(slot + 2, 7), half, z_right if slot % 2 else z_left)

    def chunk_ready(j, slot):
        if slot == 0:
            own_ready(j)
            need(*spread[j])
        else:
            need(ring[j, slot, 0], ring[j, slot, 1])

    def weights_pass(j, of):
        need(weight_far[j, of])
        block = (wo if j else wi).at[held_rows(rep, of), far_lanes]
        weight_core[j, of] = send(block, block, core)
        if (j, of) == (0, 0):
            send_block(1)
        if (j, of) == (0, 1):
            send_weights(1, 0)
            send_weights(1, 1)

    def weights_ready(j, lanes):
        for of in (0, 1):
            if lanes in (of, 2):
                own_ready((j, of))
                need(weight_core[j, of])

    stage = {}

    def quarter(of, offset=0, size=QUARTER):
        return span(((x + of) % NX) * QUARTER + offset, size, EIGHTH)

    low16, high16 = pl.ds(0, EIGHTH), pl.ds(EIGHTH, EIGHTH)

    def multiply(j, lanes, slot):
        chunk_ready(j, slot)
        weights_ready(j, lanes)
        at_lanes = pl.ds(*LANES[lanes])
        weights = (wo if j else wi)[at_lanes]
        part[j, slot, :, at_lanes] = contract(xg[j, slot], weights, 1, 1).astype(BF16)
        if (j, lanes, slot) in DIRECT:
            stage[2, j, lanes, slot] = [
                send(part.at[j, slot, quarter(of), at_lanes], target, device)
                for of, target, device in (
                    (2, across.at[j, slot, :, at_lanes], x_across),
                    (1, second.at[j, slot, 0, :, at_lanes], x_right),
                    (3, second.at[j, slot, 1, :, at_lanes], x_left),
                )
            ]
            return
        rows = (quarter(2, 0, EIGHTH), quarter(2, EIGHTH, EIGHTH))
        stage[1, j, lanes, slot] = [
            send(
                part.at[j, slot, rows[side], at_lanes],
                first.at[j, slot, side, :, at_lanes],
                x_left if side else x_right,
            )
            for side in (0, 1)
        ]

    def add_first(j, lanes, slot):
        at_lanes = pl.ds(*LANES[lanes])
        copies = []
        for side in (0, 1):
            need(stage[1, j, lanes, slot][side])
            of = 3 if side else 1
            summed = (high16, EIGHTH) if side else (low16, 0)
            plain = (low16, 0) if side else (high16, EIGHTH)
            second_out[j, slot, side, summed[0], at_lanes] = (
                part[j, slot, quarter(of, summed[1], EIGHTH), at_lanes].astype(F32)
                + first[j, slot, side, :, at_lanes].astype(F32)
            ).astype(BF16)
            second_out[j, slot, side, plain[0], at_lanes] = part[
                j, slot, quarter(of, plain[1], EIGHTH), at_lanes
            ]
            copies.append(
                send(
                    second_out.at[j, slot, side, :, at_lanes],
                    second.at[j, slot, side, :, at_lanes],
                    x_left if side else x_right,
                )
            )
        stage[2, j, lanes, slot] = copies

    def activate(j, lanes, slot):
        need(*stage[2, j, lanes, slot])
        at_lanes = pl.ds(*LANES[lanes])
        mine = quarter(0)
        total = (
            part[j, slot, mine, at_lanes].astype(F32)
            + second[j, slot, 0, :, at_lanes].astype(F32)
            + second[j, slot, 1, :, at_lanes].astype(F32)
        )
        direct = (j, lanes, slot) in DIRECT
        if direct:
            total = total + across[j, slot, :, at_lanes].astype(F32)
        if j == 0:
            bias_ready()
            value = total + bias_v[:, at_lanes]
            pre[slot, :, at_lanes] = value
            result = 0.5 * value * (1.0 + bend_of(value))
        else:
            value = pre[slot, :, at_lanes]
            bend = bend_of(value)
            slope = 0.7978845608 * (1.0 + 3.0 * 0.044715 * value * value)
            result = total * (
                0.5 * (1.0 + bend) + 0.5 * value * (1.0 - bend * bend) * slope
            )
        ap[j, slot, mine, at_lanes] = result.astype(BF16)
        if j == 1:
            hand_out(j, lanes, slot)

    def hand_out(j, lanes, slot):
        block = ap.at[j, slot, quarter(0), pl.ds(*LANES[lanes])]
        direct = (j, lanes, slot) in DIRECT
        others = [x_across] * direct + [x_right, x_left]
        stage[4 if direct else 3, j, lanes, slot] = [
            send(block, block, device) for device in others
        ]

    def hand_on(j, lanes, slot):
        at_lanes = pl.ds(*LANES[lanes])
        copies = []
        for side in (0, 1):
            need(stage[3, j, lanes, slot][side])
            rows = quarter(1, EIGHTH, EIGHTH) if side else quarter(3, 0, EIGHTH)
            block = ap.at[j, slot, rows, at_lanes]
            copies.append(send(block, block, x_left if side else x_right))
        stage[4, j, lanes, slot] = copies

    def all_here(j, lanes, slot):
        need(*stage[4, j, lanes, slot])

    core_copy, far_copy = {}, {}
    started = set()

    def weight_grad(j, lanes, pair):
        for slot in (2 * pair, 2 * pair + 1):
            chunk_ready(j, slot)
        slots, hidden = pl.ds(2 * pair, 2), pl.ds(*LANES[lanes])
        left = ap[1 - j, slots, :, hidden].reshape(2 * GROUP, LANES[lanes][1])
        right = xg[j, slots].reshape(2 * GROUP, WIDE)
        product = contract(left, right, 0, 0)
        wg[j, hidden] = wg[j, hidden] + product if (j, lanes) in started else product
        started.add((j, lanes))

    def core_send(j, of):
        rows = pl.ds(*PARTS[of])
        for far, lanes in ((1, far_lanes), (0, my_lanes)):
            block = wg[j, held_rows(1 - rep, of), lanes] * SCALE
            core_out[j, far, rows] = block.astype(BF16)
            core_copy[j, of, far] = send(
                core_out.at[j, far, rows], core_in.at[j, far, rows], core
            )

    def far_send(j, of):
        need(core_copy[j, of, 1])
        rows = pl.ds(*PARTS[of])
        block = wg[j, held_rows(rep, of), far_lanes] * SCALE
        far_out[j, rows] = (block + core_in[j, 1, rows].astype(F32)).astype(BF16)
        far_copy[j, of] = send(far_out.at[j, rows], far_in.at[j, rows], y_far)

    def weight_out(j, of):
        need(core_copy[j, of, 0], far_copy[j, of])
        rows = pl.ds(*PARTS[of])
        block = wg[j, held_rows(rep, of), my_lanes] * SCALE
        total = block + core_in[j, 0, rows].astype(F32)
        out = wgo_out if j else wgi_out
        out[rows] = (total + far_in[j, rows].astype(F32)).astype(BF16)

    bias_copy = {}

    def bias_part(slot):
        rows = ap[1, slot].astype(F32).reshape(GROUP // 8, 8, PADDED).sum(axis=0)
        bsum[...] = bsum[...] + rows if "bias" in started else rows
        started.add("bias")

    def bias_core():
        bias_copy[0] = send(bsum, bcore, core)

    def bias_far():
        need(bias_copy[0])
        bpair[...] = bsum[...] + bcore[...]
        bias_copy[1] = send(bpair, bfar, y_far)

    def bias_out():
        need(bias_copy[1])
        total = jnp.sum(bpair[...] + bfar[...], axis=0, keepdims=True) * SCALE
        mine = [
            jnp.concatenate(
                [
                    total[:, PLACE[of] + which * size : PLACE[of] + (which + 1) * size]
                    for of, (_, size) in enumerate(PARTS)
                ],
                axis=1,
            )
            for which in (0, 1)
        ]
        bg_out[...] = jnp.where(rep == 0, mine[0], mine[1])

    ring_sum, back = {}, []

    def input_part(slot):
        ig[slot] = contract(ap[1, slot], wi[...], 1, 0).astype(BF16)

    def sum_pass(side, step, half):
        slot = ((7, 6, 4, 2), (7, 5, 3, 1))[side][step]
        rows = halves[half]
        if (side, step - 1, half) in ring_sum:
            need(ring_sum[side, step - 1, half])
            ig[slot, rows] = (
                ig[slot, rows].astype(F32) + zr[side, step - 1, rows].astype(F32)
            ).astype(BF16)
        ring_sum[side, step, half] = send(
            ig.at[slot, rows], zr.at[side, step, rows], z_left if side else z_right
        )

    def sum_end():
        for half, rows in enumerate(halves):
            need(ring_sum[0, 3, half], ring_sum[1, 3, half])
            ys[rows] = (
                ig[0, rows].astype(F32)
                + zr[0, 3, rows].astype(F32)
                + zr[1, 3, rows].astype(F32)
            ).astype(BF16)
        for to_yh, to_yl, device in y_peers:
            lanes = span(to_yh * WIDTH, WIDTH, 128)
            block = ys.at[span(to_yl * HALF, HALF, HALF), lanes]
            back.append(send(block, yr.at[yh, yl], device))
        yr[yh, yl] = ys[my_rows, my_lanes]

    def input_out():
        need(*back)
        for half, rows in enumerate(halves):
            total = yr[half, 0].astype(F32) + yr[half, 1].astype(F32)
            ig_out[rows] = total.astype(BF16)

    steps = {
        "sx": begin, "zs": ring_start, "zf": ring_pass, "wf": weights_pass,
        "r1": multiply, "r2": add_first, "r3": activate, "ra": hand_out, "r4": hand_on, "r5": all_here,
        "wg": weight_grad, "cs": core_send, "fs": far_send, "wo": weight_out,
        "bp": bias_part, "bc": bias_core, "bf": bias_far, "bo": bias_out,
        "ip": input_part, "ss": sum_pass, "yb": sum_end, "io": input_out,
    }
    for name, *which in SCHEDULE:
        steps[name](*which)
    for copy in sent:
        copy.wait_send()


def hand_over(*refs):
    copies = [
        pltpu.make_async_copy(refs[n], refs[4 + n], refs[8].at[n]) for n in range(4)
    ]
    for copy in copies:
        copy.start()
    for copy in copies:
        copy.wait()


def local(tokens, out_grad, w_in, bias_in, w_out):
    hbm, vmem = pl.BlockSpec(memory_space=pl.ANY), pl.BlockSpec(memory_space=pltpu.VMEM)
    ig, wgi, bg, wgo = pl.pallas_call(
        kernel,
        name="ffn_backward",
        out_shape=(
            pltpu.VMEM((GROUP, WIDTH), BF16),
            pltpu.VMEM((CORE_HID, WIDTH), BF16),
            pltpu.VMEM((1, CORE_HID), F32),
            pltpu.VMEM((CORE_HID, WIDTH), BF16),
        ),
        in_specs=[hbm] * 5,
        out_specs=(vmem,) * 4,
        scratch_shapes=[
            pltpu.VMEM((2, CHUNKS, GROUP, WIDE), BF16),
            pltpu.VMEM((PADDED, WIDE), BF16),
            pltpu.VMEM((PADDED, WIDE), BF16),
            pltpu.VMEM((HID,), F32),
            pltpu.VMEM((1, PADDED), F32),
            pltpu.VMEM((2, CHUNKS, GROUP, PADDED), BF16),
            pltpu.VMEM((2, CHUNKS, 2, EIGHTH, PADDED), BF16),
            pltpu.VMEM((2, CHUNKS, 2, QUARTER, PADDED), BF16),
            pltpu.VMEM((2, CHUNKS, 2, QUARTER, PADDED), BF16),
            pltpu.VMEM((2, CHUNKS, QUARTER, PADDED), BF16),
            pltpu.VMEM((2, CHUNKS, GROUP, PADDED), BF16),
            pltpu.VMEM((CHUNKS, QUARTER, PADDED), F32),
            pltpu.VMEM((CHUNKS, GROUP, WIDE), BF16),
            pltpu.VMEM((2, 4, GROUP, WIDE), BF16),
            pltpu.VMEM((GROUP, WIDE), BF16),
            pltpu.VMEM((2, 2, HALF, WIDTH), BF16),
            pltpu.VMEM((2, PADDED, WIDE), F32),
            pltpu.VMEM((2, 2, CORE_HID, WIDTH), BF16),
            pltpu.VMEM((2, 2, CORE_HID, WIDTH), BF16),
            pltpu.VMEM((2, CORE_HID, WIDTH), BF16),
            pltpu.VMEM((2, CORE_HID, WIDTH), BF16),
            pltpu.VMEM((8, PADDED), F32),
            pltpu.VMEM((8, PADDED), F32),
            pltpu.VMEM((8, PADDED), F32),
            pltpu.VMEM((8, PADDED), F32),
            pltpu.SemaphoreType.DMA((11,)),
            pltpu.SemaphoreType.DMA((360,)),
            pltpu.SemaphoreType.DMA((360,)),
        ],
        compiler_params=pltpu.CompilerParams(
            collective_id=0, has_side_effects=True, vmem_limit_bytes=58 << 20
        ),
        cost_estimate=pl.CostEstimate(
            flops=11_300_000_000, bytes_accessed=4_000_000, transcendentals=0
        ),
    )(tokens, out_grad, w_in.T, bias_in, w_out)
    ig, wgi, bg, wgo = pl.pallas_call(
        hand_over,
        name="hand_over",
        out_shape=tuple(jax.ShapeDtypeStruct(v.shape, v.dtype) for v in (ig, wgi, bg, wgo)),
        in_specs=[vmem] * 4,
        out_specs=(hbm,) * 4,
        scratch_shapes=[pltpu.SemaphoreType.DMA((4,))],
    )(*(pltpu.with_memory_space_constraint(v, pltpu.VMEM) for v in (ig, wgi, bg, wgo)))
    return ig, wgi.T, bg.reshape(CORE_HID), wgo


def solution(mesh):
    in_specs = (
        P(("col", "rep"), "row"),
        P(("col", "rep"), "row"),
        P("row", "col"),
        P("col"),
        P("col", "row"),
    )
    out_specs = (
        P(("col", "rep"), "row"),
        P("row", ("col", "rep")),
        P(("col", "rep")),
        P(("col", "rep"), "row"),
    )
    return jax.shard_map(local, mesh=mesh, in_specs=in_specs, out_specs=out_specs, check_vma=False)
```

```python
import jax
import jax.numpy as jnp
from jax import lax
from jax.experimental import pallas as pl
from jax.experimental.pallas import tpu as pltpu
from jax.sharding import PartitionSpec as P

MESH = pl.DeviceIdType.MESH
BF16, F32 = jnp.bfloat16, jnp.float32
NX, NZ = 4, 8
GROUP, HALF = 128, 64
WIDTH, WIDE = 640, 1280
HID, CORE_HID = 864, 432
PADDED = 896
PARTS = ((0, 192), (192, 240))
PLACE = (0, 384)
LANES = ((0, 384), (384, 512), (0, 896))
QUARTER, EIGHTH = 32, 16
CHUNKS = 8
SCALE = 1.0 / 64.0
DIRECT = ((1, 0, 7), (1, 1, 7))
SCHEDULE = (
    ("sx",), ("zs", 0), ("wf", 0, 0), ("zf", 0, 1, 0), ("zf", 0, 2, 1), ("r1", 0, 0, 0), ("r1", 0, 0, 1),
    ("zf", 0, 2, 0), ("zf", 0, 1, 1), ("r1", 0, 0, 2), ("r2", 0, 0, 0), ("wf", 0, 1), ("zf", 0, 3, 0),
    ("zf", 0, 4, 1), ("r2", 0, 0, 1), ("r2", 0, 0, 2), ("r1", 0, 1, 0), ("r3", 0, 0, 0), ("ra", 0, 0, 0),
    ("r1", 0, 1, 1), ("r1", 0, 1, 2), ("r1", 0, 0, 3), ("r3", 0, 0, 1), ("ra", 0, 0, 1), ("zf", 0, 4, 0),
    ("zf", 0, 3, 1), ("r3", 0, 0, 2), ("ra", 0, 0, 2), ("r1", 0, 1, 3), ("r2", 0, 1, 0), ("r4", 0, 0, 0),
    ("r1", 0, 0, 4), ("r2", 0, 1, 1), ("r2", 0, 1, 2), ("zf", 0, 5, 0), ("zf", 0, 6, 1), ("r2", 0, 0, 3),
    ("zs", 1), ("r4", 0, 0, 1), ("wf", 1, 0), ("r4", 0, 0, 2), ("r1", 0, 1, 4), ("r2", 0, 1, 3),
    ("r3", 0, 1, 0), ("ra", 0, 1, 0), ("r5", 0, 0, 0), ("r2", 0, 0, 4), ("r1", 0, 1, 5), ("r1", 1, 0, 0),
    ("r1", 0, 0, 6), ("r3", 0, 0, 3), ("r5", 0, 0, 1), ("ra", 0, 0, 3), ("r1", 0, 0, 5), ("r5", 0, 0, 2),
    ("r2", 0, 1, 4), ("r1", 0, 1, 6), ("wf", 1, 1), ("r1", 0, 0, 7), ("r4", 0, 1, 0), ("r1", 0, 1, 7),
    ("r3", 0, 0, 4), ("r2", 0, 1, 5), ("ra", 0, 0, 4), ("r2", 1, 0, 0), ("r2", 0, 0, 6), ("r3", 0, 1, 3),
    ("r3", 0, 1, 2), ("r3", 0, 1, 1), ("r4", 0, 0, 3), ("r2", 0, 0, 5), ("zf", 1, 1, 0), ("zf", 1, 2, 1),
    ("r3", 0, 1, 4), ("ra", 0, 1, 3), ("r2", 0, 1, 6), ("r2", 0, 0, 7), ("r5", 0, 1, 0), ("r2", 0, 1, 7),
    ("r3", 0, 1, 5), ("r4", 0, 0, 4), ("zf", 1, 1, 1), ("zf", 1, 2, 0), ("r3", 1, 0, 0), ("r3", 0, 0, 6),
    ("ra", 0, 0, 6), ("r5", 0, 0, 3), ("ra", 0, 1, 1), ("r3", 0, 0, 5), ("ra", 0, 0, 5), ("r4", 0, 1, 3),
    ("r1", 1, 0, 1), ("zf", 1, 4, 1), ("r3", 0, 1, 6), ("ra", 0, 1, 6), ("zf", 1, 3, 0), ("r3", 0, 0, 7),
    ("ra", 0, 0, 7), ("r3", 0, 1, 7), ("ra", 0, 1, 2), ("r5", 0, 0, 4), ("r4", 1, 0, 0), ("ra", 0, 1, 4),
    ("r4", 0, 0, 6), ("r4", 0, 1, 1), ("zf", 1, 3, 1), ("zf", 1, 4, 0), ("r1", 1, 0, 4), ("r5", 0, 1, 3),
    ("r1", 1, 0, 3), ("r2", 1, 0, 1), ("r1", 1, 1, 4), ("ra", 0, 1, 5), ("r4", 0, 0, 7), ("r4", 0, 1, 6),
    ("r4", 0, 0, 5), ("r4", 0, 1, 2), ("r5", 1, 0, 0), ("zf", 1, 5, 0), ("zf", 1, 6, 1), ("ra", 0, 1, 7),
    ("r4", 0, 1, 4), ("r5", 0, 0, 6), ("r5", 0, 1, 1), ("wg", 1, 2, 0), ("r3", 1, 0, 1), ("r2", 1, 0, 4),
    ("r1", 1, 1, 3), ("r1", 1, 1, 5), ("r5", 0, 0, 7), ("r5", 0, 1, 6), ("r1", 1, 0, 6), ("r4", 0, 1, 5),
    ("r5", 0, 0, 5), ("r1", 1, 1, 6), ("r4", 0, 1, 7), ("r1", 1, 0, 5), ("r5", 0, 1, 4), ("r1", 1, 0, 2),
    ("r4", 1, 0, 1), ("r1", 1, 0, 7), ("r1", 1, 1, 7), ("r2", 1, 1, 5), ("r2", 1, 0, 6), ("r5", 0, 1, 5),
    ("wg", 1, 2, 2), ("r2", 1, 1, 6), ("r2", 1, 0, 5), ("r5", 0, 1, 7), ("wg", 1, 2, 3), ("r3", 1, 0, 7),
    ("r5", 1, 0, 1), ("wg", 0, 0, 0), ("r3", 1, 1, 7), ("r5", 0, 1, 2), ("wg", 1, 2, 1), ("r3", 1, 0, 6),
    ("r3", 1, 1, 6), ("cs", 1, 1), ("r3", 1, 1, 5), ("r3", 1, 0, 5), ("cs", 1, 0), ("r3", 1, 0, 4),
    ("r5", 1, 0, 7), ("r2", 1, 1, 4), ("r2", 1, 0, 3), ("r2", 1, 1, 3), ("r2", 1, 0, 2), ("fs", 1, 1),
    ("r5", 1, 1, 7), ("ip", 7), ("ss", 0, 0, 0), ("r4", 1, 0, 6), ("fs", 1, 0), ("ss", 1, 0, 1),
    ("r4", 1, 1, 6), ("bp", 7), ("r1", 1, 1, 2), ("r4", 1, 0, 5), ("r4", 1, 1, 5), ("r1", 1, 1, 1),
    ("r1", 1, 1, 0), ("r3", 1, 1, 4), ("r3", 1, 0, 3), ("r4", 1, 0, 4), ("r3", 1, 1, 3), ("r3", 1, 0, 2),
    ("r5", 1, 0, 6), ("wg", 0, 0, 3), ("r5", 1, 1, 6), ("ip", 6), ("ss", 0, 1, 1), ("r5", 1, 0, 5),
    ("r2", 1, 1, 2), ("r5", 1, 1, 5), ("ip", 5), ("ss", 1, 1, 0), ("ss", 1, 1, 1), ("r2", 1, 1, 1),
    ("r4", 1, 1, 4), ("wg", 0, 1, 3), ("r4", 1, 0, 3), ("bp", 5), ("wo", 1, 1), ("bp", 6), ("r4", 1, 1, 3),
    ("r2", 1, 1, 0), ("r5", 1, 0, 4), ("ss", 0, 1, 0), ("r4", 1, 0, 2), ("wg", 0, 0, 2), ("r3", 1, 1, 2),
    ("r3", 1, 1, 1), ("r5", 1, 1, 4), ("ip", 4), ("ss", 0, 2, 1), ("bp", 4), ("r5", 1, 1, 3),
    ("r5", 1, 0, 3), ("ip", 3), ("ss", 1, 2, 0), ("r3", 1, 1, 0), ("r5", 1, 0, 2), ("wg", 0, 0, 1),
    ("r4", 1, 1, 2), ("bp", 3), ("cs", 0, 0), ("wo", 1, 0), ("r4", 1, 1, 1), ("wg", 0, 1, 2),
    ("ss", 0, 2, 0), ("ss", 1, 2, 1), ("fs", 0, 0), ("r4", 1, 1, 0), ("r5", 1, 1, 2), ("ip", 2), ("bp", 2),
    ("wg", 0, 1, 1), ("ss", 0, 3, 1), ("r5", 1, 1, 1), ("ip", 1), ("bp", 1), ("ss", 1, 3, 0),
    ("r5", 1, 1, 0), ("bp", 0), ("bc",), ("wg", 0, 1, 0), ("cs", 0, 1), ("ip", 0), ("bf",), ("ss", 0, 3, 0),
    ("ss", 1, 3, 1), ("fs", 0, 1), ("wo", 0, 0), ("bo",), ("yb",), ("wo", 0, 1), ("io",),
)


def contract(a, b, dim_a, dim_b):
    return lax.dot_general(
        a, b, (((dim_a,), (dim_b,)), ((), ())), preferred_element_type=F32
    )


def bend_of(value):
    return jnp.tanh(0.7978845608 * (value + 0.044715 * value * value * value))


def kernel(
    tok, og, win, bias, wout,
    ig_out, wgi_out, bg_out, wgo_out,
    xg, wi, wo, bias_raw, bias_v, part, first, second_out, second, across, ap, pre,
    ig, zr, ys, yr, wg, core_out, core_in, far_out, far_in,
    bsum, bcore, bpair, bfar,
    local_sem, send_sem, recv_sem,
):
    row, col, rep = lax.axis_index("row"), lax.axis_index("col"), lax.axis_index("rep")
    yh, x = row // NX, row % NX
    yl, z = col // NZ, col % NZ

    def at(yh_=yh, x_=x, yl_=yl, z_=z, rep_=rep):
        return {"row": yh_ * NX + x_, "col": yl_ * NZ + z_, "rep": rep_}

    x_right, x_left = at(x_=(x + 1) % NX), at(x_=(x + 3) % NX)
    x_across = at(x_=(x + 2) % NX)
    z_right, z_left = at(z_=(z + 1) % NZ), at(z_=(z + 7) % NZ)
    core = at(rep_=1 - rep)
    y_far = at(yh_=1 - yh)
    y_peers = [
        (1 - yh, yl, y_far),
        (1 - yh, 1 - yl, at(yh_=1 - yh, yl_=1 - yl)),
        (yh, 1 - yl, at(yl_=1 - yl)),
    ]

    counts = {"local": 0, "remote": 0}
    sent, arrived = [], set()

    def move(src, dst):
        copy = pltpu.make_async_copy(src, dst, local_sem.at[counts["local"]])
        counts["local"] += 1
        copy.start()
        return copy

    def send(src, dst, device):
        number = counts["remote"]
        counts["remote"] += 1
        copy = pltpu.make_async_remote_copy(
            src_ref=src,
            dst_ref=dst,
            send_sem=send_sem.at[number],
            recv_sem=recv_sem.at[number],
            device_id=device,
            device_id_type=MESH,
        )
        copy.start()
        sent.append(copy)
        return copy

    def need(*copies):
        for copy in copies:
            if id(copy) not in arrived:
                arrived.add(id(copy))
                copy.wait_recv()

    def span(start, size, unit):
        return pl.ds(pl.multiple_of(start, unit), size)

    my_rows = span(yl * HALF, HALF, HALF)
    my_lanes = span(yh * WIDTH, WIDTH, 128)
    far_lanes = span((1 - yh) * WIDTH, WIDTH, 128)

    def source_rows(which, of):
        start, size = PARTS[of]
        return span(which * CORE_HID + start, size, 16)

    def held_rows(which, of):
        size = PARTS[of][1]
        return span(PLACE[of] + which * size, size, 16)

    barrier = pltpu.get_barrier_semaphore()
    everyone = [x_right, x_left, x_across, z_right, z_left, core] + [p[2] for p in y_peers]
    for device in everyone:
        pl.semaphore_signal(barrier, inc=1, device_id=device, device_id_type=MESH)

    own = {}
    for j, (block, weights, held) in enumerate(((tok, win, wi), (og, wout, wo))):
        own[j] = [
            move(block.at[span(yh * HALF, HALF, HALF)], xg.at[j, 0, my_rows, my_lanes])
        ]
        for of in (0, 1):
            own[j, of] = [
                move(
                    weights.at[pl.ds(which * CORE_HID + PARTS[of][0], PARTS[of][1])],
                    held.at[
                        pl.ds(PLACE[of] + which * PARTS[of][1], PARTS[of][1]), my_lanes
                    ],
                )
                for which in (0, 1)
            ]
    own_bias = [move(bias, bias_raw)]

    def own_ready(key):
        while own[key]:
            own[key].pop().wait()

    own["bias"] = own_bias

    def bias_ready():
        if not own["bias"]:
            return
        own_ready("bias")
        raw = bias_raw[...].reshape(1, HID)
        blocks = [
            raw[:, which * CORE_HID + start : which * CORE_HID + start + size]
            for start, size in PARTS
            for which in (0, 1)
        ]
        blocks.append(jnp.zeros((1, PADDED - HID), F32))
        bias_v[...] = jnp.concatenate(blocks, axis=1)

    for held in (wi, wo):
        held[pl.ds(HID, PADDED - HID)] = jnp.zeros((PADDED - HID, WIDE), BF16)

    pl.semaphore_wait(barrier, len(everyone))

    spread, weight_far, weight_core, ring = {}, {}, {}, {}
    halves = (pl.ds(0, HALF), pl.ds(HALF, HALF))

    def send_block(j):
        source = og if j else tok
        spread[j] = [
            send(
                source.at[span(to_yh * HALF, HALF, HALF)],
                xg.at[j, 0, my_rows, my_lanes],
                device,
            )
            for to_yh, _, device in y_peers
        ]

    def send_weights(j, of):
        source, held = (wout, wo) if j else (win, wi)
        weight_far[j, of] = send(
            source.at[source_rows(rep, of)], held.at[held_rows(rep, of), my_lanes], y_far
        )

    def begin():
        send_block(0)
        send_weights(0, 0)

    def ring_send(j, source, slot, half, device):
        rows = halves[half]
        ring[j, slot, half] = send(xg.at[j, source, rows], xg.at[j, slot, rows], device)

    def ring_start(j):
        own_ready(j)
        need(*spread[j])
        for half in (0, 1):
            ring_send(j, 0, 1, half, z_right)
            ring_send(j, 0, 2, 1 - half, z_left)
        if j == 0:
            send_weights(0, 1)

    def ring_pass(j, slot, half):
        need(ring[j, slot, half])
        ring_send(j, slot, min(slot + 2, 7), half, z_right if slot % 2 else z_left)

    def chunk_ready(j, slot):
        if slot == 0:
            own_ready(j)
            need(*spread[j])
        else:
            need(ring[j, slot, 0], ring[j, slot, 1])

    def weights_pass(j, of):
        need(weight_far[j, of])
        block = (wo if j else wi).at[held_rows(rep, of), far_lanes]
        weight_core[j, of] = send(block, block, core)
        if (j, of) == (0, 0):
            send_block(1)
        if (j, of) == (0, 1):
            send_weights(1, 0)
            send_weights(1, 1)

    def weights_ready(j, lanes):
        for of in (0, 1):
            if lanes in (of, 2):
                own_ready((j, of))
                need(weight_core[j, of])

    stage = {}

    def quarter(of, offset=0, size=QUARTER):
        return span(((x + of) % NX) * QUARTER + offset, size, EIGHTH)

    low16, high16 = pl.ds(0, EIGHTH), pl.ds(EIGHTH, EIGHTH)

    def multiply(j, lanes, slot):
        chunk_ready(j, slot)
        weights_ready(j, lanes)
        at_lanes = pl.ds(*LANES[lanes])
        weights = (wo if j else wi)[at_lanes]
        part[j, slot, :, at_lanes] = contract(xg[j, slot], weights, 1, 1).astype(BF16)
        if (j, lanes, slot) in DIRECT:
            stage[2, j, lanes, slot] = [
                send(part.at[j, slot, quarter(of), at_lanes], target, device)
                for of, target, device in (
                    (2, across.at[j, slot, :, at_lanes], x_across),
                    (1, second.at[j, slot, 0, :, at_lanes], x_right),
                    (3, second.at[j, slot, 1, :, at_lanes], x_left),
                )
            ]
            return
        rows = (quarter(2, 0, EIGHTH), quarter(2, EIGHTH, EIGHTH))
        stage[1, j, lanes, slot] = [
            send(
                part.at[j, slot, rows[side], at_lanes],
                first.at[j, slot, side, :, at_lanes],
                x_left if side else x_right,
            )
            for side in (0, 1)
        ]

    def add_first(j, lanes, slot):
        at_lanes = pl.ds(*LANES[lanes])
        copies = []
        for side in (0, 1):
            need(stage[1, j, lanes, slot][side])
            of = 3 if side else 1
            summed = (high16, EIGHTH) if side else (low16, 0)
            plain = (low16, 0) if side else (high16, EIGHTH)
            second_out[j, slot, side, summed[0], at_lanes] = (
                part[j, slot, quarter(of, summed[1], EIGHTH), at_lanes].astype(F32)
                + first[j, slot, side, :, at_lanes].astype(F32)
            ).astype(BF16)
            second_out[j, slot, side, plain[0], at_lanes] = part[
                j, slot, quarter(of, plain[1], EIGHTH), at_lanes
            ]
            copies.append(
                send(
                    second_out.at[j, slot, side, :, at_lanes],
                    second.at[j, slot, side, :, at_lanes],
                    x_left if side else x_right,
                )
            )
        stage[2, j, lanes, slot] = copies

    def activate(j, lanes, slot):
        need(*stage[2, j, lanes, slot])
        at_lanes = pl.ds(*LANES[lanes])
        mine = quarter(0)
        total = (
            part[j, slot, mine, at_lanes].astype(F32)
            + second[j, slot, 0, :, at_lanes].astype(F32)
            + second[j, slot, 1, :, at_lanes].astype(F32)
        )
        direct = (j, lanes, slot) in DIRECT
        if direct:
            total = total + across[j, slot, :, at_lanes].astype(F32)
        if j == 0:
            bias_ready()
            value = total + bias_v[:, at_lanes]
            pre[slot, :, at_lanes] = value
            result = 0.5 * value * (1.0 + bend_of(value))
        else:
            value = pre[slot, :, at_lanes]
            bend = bend_of(value)
            slope = 0.7978845608 * (1.0 + 3.0 * 0.044715 * value * value)
            result = total * (
                0.5 * (1.0 + bend) + 0.5 * value * (1.0 - bend * bend) * slope
            )
        ap[j, slot, mine, at_lanes] = result.astype(BF16)
        if j == 1:
            hand_out(j, lanes, slot)

    def hand_out(j, lanes, slot):
        block = ap.at[j, slot, quarter(0), pl.ds(*LANES[lanes])]
        direct = (j, lanes, slot) in DIRECT
        others = [x_across] * direct + [x_right, x_left]
        stage[4 if direct else 3, j, lanes, slot] = [
            send(block, block, device) for device in others
        ]

    def hand_on(j, lanes, slot):
        at_lanes = pl.ds(*LANES[lanes])
        copies = []
        for side in (0, 1):
            need(stage[3, j, lanes, slot][side])
            rows = quarter(1, EIGHTH, EIGHTH) if side else quarter(3, 0, EIGHTH)
            block = ap.at[j, slot, rows, at_lanes]
            copies.append(send(block, block, x_left if side else x_right))
        stage[4, j, lanes, slot] = copies

    def all_here(j, lanes, slot):
        need(*stage[4, j, lanes, slot])

    core_copy, far_copy = {}, {}
    started = set()

    def weight_grad(j, lanes, pair):
        for slot in (2 * pair, 2 * pair + 1):
            chunk_ready(j, slot)
        slots, hidden = pl.ds(2 * pair, 2), pl.ds(*LANES[lanes])
        left = ap[1 - j, slots, :, hidden].reshape(2 * GROUP, LANES[lanes][1])
        right = xg[j, slots].reshape(2 * GROUP, WIDE)
        product = contract(left, right, 0, 0)
        wg[j, hidden] = wg[j, hidden] + product if (j, lanes) in started else product
        started.add((j, lanes))

    def core_send(j, of):
        rows = pl.ds(*PARTS[of])
        for far, lanes in ((1, far_lanes), (0, my_lanes)):
            block = wg[j, held_rows(1 - rep, of), lanes] * SCALE
            core_out[j, far, rows] = block.astype(BF16)
            core_copy[j, of, far] = send(
                core_out.at[j, far, rows], core_in.at[j, far, rows], core
            )

    def far_send(j, of):
        need(core_copy[j, of, 1])
        rows = pl.ds(*PARTS[of])
        block = wg[j, held_rows(rep, of), far_lanes] * SCALE
        far_out[j, rows] = (block + core_in[j, 1, rows].astype(F32)).astype(BF16)
        far_copy[j, of] = send(far_out.at[j, rows], far_in.at[j, rows], y_far)

    def weight_out(j, of):
        need(core_copy[j, of, 0], far_copy[j, of])
        rows = pl.ds(*PARTS[of])
        block = wg[j, held_rows(rep, of), my_lanes] * SCALE
        total = block + core_in[j, 0, rows].astype(F32)
        out = wgo_out if j else wgi_out
        out[rows] = (total + far_in[j, rows].astype(F32)).astype(BF16)

    bias_copy = {}

    def bias_part(slot):
        rows = ap[1, slot].astype(F32).reshape(GROUP // 8, 8, PADDED).sum(axis=0)
        bsum[...] = bsum[...] + rows if "bias" in started else rows
        started.add("bias")

    def bias_core():
        bias_copy[0] = send(bsum, bcore, core)

    def bias_far():
        need(bias_copy[0])
        bpair[...] = bsum[...] + bcore[...]
        bias_copy[1] = send(bpair, bfar, y_far)

    def bias_out():
        need(bias_copy[1])
        total = jnp.sum(bpair[...] + bfar[...], axis=0, keepdims=True) * SCALE
        mine = [
            jnp.concatenate(
                [
                    total[:, PLACE[of] + which * size : PLACE[of] + (which + 1) * size]
                    for of, (_, size) in enumerate(PARTS)
                ],
                axis=1,
            )
            for which in (0, 1)
        ]
        bg_out[...] = jnp.where(rep == 0, mine[0], mine[1])

    ring_sum, back = {}, []

    def input_part(slot):
        ig[slot] = contract(ap[1, slot], wi[...], 1, 0).astype(BF16)

    def sum_pass(side, step, half):
        slot = ((7, 6, 4, 2), (7, 5, 3, 1))[side][step]
        rows = halves[half]
        if (side, step - 1, half) in ring_sum:
            need(ring_sum[side, step - 1, half])
            ig[slot, rows] = (
                ig[slot, rows].astype(F32) + zr[side, step - 1, rows].astype(F32)
            ).astype(BF16)
        ring_sum[side, step, half] = send(
            ig.at[slot, rows], zr.at[side, step, rows], z_left if side else z_right
        )

    def sum_end():
        for half, rows in enumerate(halves):
            need(ring_sum[0, 3, half], ring_sum[1, 3, half])
            ys[rows] = (
                ig[0, rows].astype(F32)
                + zr[0, 3, rows].astype(F32)
                + zr[1, 3, rows].astype(F32)
            ).astype(BF16)
        for to_yh, to_yl, device in y_peers:
            lanes = span(to_yh * WIDTH, WIDTH, 128)
            block = ys.at[span(to_yl * HALF, HALF, HALF), lanes]
            back.append(send(block, yr.at[yh, yl], device))
        yr[yh, yl] = ys[my_rows, my_lanes]

    def input_out():
        need(*back)
        for half, rows in enumerate(halves):
            total = yr[half, 0].astype(F32) + yr[half, 1].astype(F32)
            ig_out[rows] = total.astype(BF16)

    steps = {
        "sx": begin, "zs": ring_start, "zf": ring_pass, "wf": weights_pass,
        "r1": multiply, "r2": add_first, "r3": activate, "ra": hand_out, "r4": hand_on, "r5": all_here,
        "wg": weight_grad, "cs": core_send, "fs": far_send, "wo": weight_out,
        "bp": bias_part, "bc": bias_core, "bf": bias_far, "bo": bias_out,
        "ip": input_part, "ss": sum_pass, "yb": sum_end, "io": input_out,
    }
    for name, *which in SCHEDULE:
        steps[name](*which)
    for copy in sent:
        copy.wait_send()


def hand_over(*refs):
    copies = [
        pltpu.make_async_copy(refs[n], refs[4 + n], refs[8].at[n]) for n in range(4)
    ]
    for copy in copies:
        copy.start()
    for copy in copies:
        copy.wait()


def local(tokens, out_grad, w_in, bias_in, w_out):
    hbm, vmem = pl.BlockSpec(memory_space=pl.ANY), pl.BlockSpec(memory_space=pltpu.VMEM)
    ig, wgi, bg, wgo = pl.pallas_call(
        kernel,
        name="ffn_backward",
        out_shape=(
            pltpu.VMEM((GROUP, WIDTH), BF16),
            pltpu.VMEM((CORE_HID, WIDTH), BF16),
            pltpu.VMEM((1, CORE_HID), F32),
            pltpu.VMEM((CORE_HID, WIDTH), BF16),
        ),
        in_specs=[hbm] * 5,
        out_specs=(vmem,) * 4,
        scratch_shapes=[
            pltpu.VMEM((2, CHUNKS, GROUP, WIDE), BF16),
            pltpu.VMEM((PADDED, WIDE), BF16),
            pltpu.VMEM((PADDED, WIDE), BF16),
            pltpu.VMEM((HID,), F32),
            pltpu.VMEM((1, PADDED), F32),
            pltpu.VMEM((2, CHUNKS, GROUP, PADDED), BF16),
            pltpu.VMEM((2, CHUNKS, 2, EIGHTH, PADDED), BF16),
            pltpu.VMEM((2, CHUNKS, 2, QUARTER, PADDED), BF16),
            pltpu.VMEM((2, CHUNKS, 2, QUARTER, PADDED), BF16),
            pltpu.VMEM((2, CHUNKS, QUARTER, PADDED), BF16),
            pltpu.VMEM((2, CHUNKS, GROUP, PADDED), BF16),
            pltpu.VMEM((CHUNKS, QUARTER, PADDED), F32),
            pltpu.VMEM((CHUNKS, GROUP, WIDE), BF16),
            pltpu.VMEM((2, 4, GROUP, WIDE), BF16),
            pltpu.VMEM((GROUP, WIDE), BF16),
            pltpu.VMEM((2, 2, HALF, WIDTH), BF16),
            pltpu.VMEM((2, PADDED, WIDE), F32),
            pltpu.VMEM((2, 2, CORE_HID, WIDTH), BF16),
            pltpu.VMEM((2, 2, CORE_HID, WIDTH), BF16),
            pltpu.VMEM((2, CORE_HID, WIDTH), BF16),
            pltpu.VMEM((2, CORE_HID, WIDTH), BF16),
            pltpu.VMEM((8, PADDED), F32),
            pltpu.VMEM((8, PADDED), F32),
            pltpu.VMEM((8, PADDED), F32),
            pltpu.VMEM((8, PADDED), F32),
            pltpu.SemaphoreType.DMA((11,)),
            pltpu.SemaphoreType.DMA((360,)),
            pltpu.SemaphoreType.DMA((360,)),
        ],
        compiler_params=pltpu.CompilerParams(
            collective_id=0, has_side_effects=True, vmem_limit_bytes=58 << 20
        ),
        cost_estimate=pl.CostEstimate(
            flops=11_300_000_000, bytes_accessed=4_000_000, transcendentals=0
        ),
    )(tokens, out_grad, w_in.T, bias_in, w_out)
    ig, wgi, bg, wgo = pl.pallas_call(
        hand_over,
        name="hand_over",
        out_shape=tuple(jax.ShapeDtypeStruct(v.shape, v.dtype) for v in (ig, wgi, bg, wgo)),
        in_specs=[vmem] * 4,
        out_specs=(hbm,) * 4,
        scratch_shapes=[pltpu.SemaphoreType.DMA((4,))],
    )(*(pltpu.with_memory_space_constraint(v, pltpu.VMEM) for v in (ig, wgi, bg, wgo)))
    return ig, wgi.T, bg.reshape(CORE_HID), wgo


def solution(mesh):
    in_specs = (
        P(("col", "rep"), "row"),
        P(("col", "rep"), "row"),
        P("row", "col"),
        P("col"),
        P("col", "row"),
    )
    out_specs = (
        P(("col", "rep"), "row"),
        P("row", ("col", "rep")),
        P(("col", "rep")),
        P(("col", "rep"), "row"),
    )
    return jax.shard_map(local, mesh=mesh, in_specs=in_specs, out_specs=out_specs, check_vma=False)
```
